512 devices in a mesh: ens: 8 (over y), sy: 8 (over z), sx: 8 (over x, core).
Axes of the slice: x: 4, y: 8, z: 8, core: 2. Of those that a mesh axis runs over, the one named last changes fastest.
Arguments:
- fine_state: bfloat16 [8, 16, 16, 128, 256], P('ens', 'sy', 'sx'), may hold values from -6 to 6
- fine_adj: bfloat16 [16, 16, 4, 128, 128], P('sy', 'sx'), may hold values from -0.25 to 0.25
- fine_nbr: int32 [16, 16, 4], P('sy', 'sx'), may hold values from 0 to 8
- up_map: int32 [16, 16], P('sy', 'sx'), may hold values from 0 to 19
- up_tiles: bfloat16 [16, 16, 128, 128], P('sy', 'sx'), may hold values from -0.5 to 0.5
- top_adj: bfloat16 [20, 4, 128, 128], replicated, may hold values from -0.25 to 0.25
- top_nbr: int32 [20, 4], replicated, may hold values from 0 to 19
- w_fine_msg: bfloat16 [256, 256], replicated, may hold values from -0.375 to 0.375
- w_fine_self: bfloat16 [256, 256], replicated, may hold values from -0.375 to 0.375
- w_fine_agg: bfloat16 [256, 256], replicated, may hold values from -0.375 to 0.375
- w_fine_out: bfloat16 [256, 256], replicated, may hold values from -0.375 to 0.375
- w_top_msg: bfloat16 [256, 256], replicated, may hold values from -0.375 to 0.375
- w_top_agg: bfloat16 [256, 256], replicated, may hold values from -0.375 to 0.375
- w_down: bfloat16 [256, 256], replicated, may hold values from -0.375 to 0.375
- fine_gain: float32 [256], replicated, may hold values from 0.25 to 1.75
- top_gain: float32 [256], replicated, may hold values from 0.25 to 1.75
- out_gain: float32 [256], replicated, may hold values from 0.25 to 1.75
Outputs:
- fine_out: bfloat16 [8, 16, 16, 128, 256], P('ens', 'sy', 'sx')
The draws below stay inside these ranges and needn't reach their ends.
Inputs may be any that keep to these rules, and one draw needn't show every extreme that they name: `fine_nbr`: code v names the block at offset (v // 3 - 1, v % 3 - 1) in (latitude, longitude).
All inputs are finite; a program needn't handle non-finite values.
Results may differ from the reference program's by a relative error of at most 0.015.
Values may be sent and summed in bfloat16 or wider, within the bound.
No kernel may reach another device: no remote copies, remote signals or barrier semaphores. Data moves between devices by JAX's collectives and lax.ppermute only.
A program may use at most 64 MiB of HBM per device.

```python
import jax
import jax.numpy as jnp
from jax import lax

WIDTH = 256
BLOCK = 128
NBR = 4
TOP_BLK = 20
TOP_NBR = 4
MEMBERS = 8
FINE_Y = 16
FINE_X = 16


def place_ends(values, key, low, high):
    dims = values.shape
    spot = [jax.random.randint(jax.random.fold_in(key, axis), (), 0, dims[axis]) for axis in range(len(dims))]
    values = values.at[tuple(spot)].set(low)
    longest = dims.index(max(dims))
    spot[longest] = (spot[longest] + 1) % dims[longest]
    return values.at[tuple(spot)].set(high)


def block_scale(own_key, dims, pieces, low, top_value):
    level, own = 1.0, jax.random.fold_in(own_key, 6)
    for axis_at, parts in pieces:
        heights = jnp.exp(jax.random.uniform(jax.random.fold_in(own, axis_at), (parts,), jnp.float32, low / len(pieces), top_value / len(pieces)))
        level = level * jnp.repeat(heights, dims[axis_at] // parts).reshape([-1 if axis == axis_at else 1 for axis in range(len(dims))])
    return level


def bell_draw(rng, dims, width, reach, pieces=(), kind=jnp.bfloat16):
    loudness = block_scale(rng, dims, pieces, -0.22, 0.18) if pieces else 1.0
    values = jax.random.normal(rng, dims, jnp.float32) * width * loudness
    return jnp.minimum(jnp.maximum(values, -reach), reach).astype(kind)


def setup_inputs(seed: int = 0) -> dict:
    streams_of = jax.random.split(jax.random.key(seed), 18)
    fine_state = bell_draw(streams_of[0], (MEMBERS, FINE_Y, FINE_X, BLOCK, WIDTH), 1.0, 6.0, ((0, 8), (1, 8), (2, 8)))
    fine_adj = bell_draw(streams_of[1], (FINE_Y, FINE_X, NBR, BLOCK, BLOCK), (NBR * BLOCK) ** -0.5, 0.25, ((0, 8), (1, 8)))
    fine_nbr = place_ends(jax.random.randint(streams_of[2], (FINE_Y, FINE_X, NBR), 0, 9), jax.random.fold_in(streams_of[2], 1), 0, 8).astype(jnp.int32)
    up_map = place_ends(jax.random.randint(streams_of[3], (FINE_Y, FINE_X), 0, TOP_BLK), jax.random.fold_in(streams_of[3], 1), 0, TOP_BLK - 1).astype(jnp.int32)
    up_tiles = bell_draw(streams_of[4], (FINE_Y, FINE_X, BLOCK, BLOCK), BLOCK ** -0.5, 0.5, ((0, 8), (1, 8)))
    top_adj = bell_draw(streams_of[5], (TOP_BLK, TOP_NBR, BLOCK, BLOCK), (TOP_NBR * BLOCK) ** -0.5, 0.25)
    top_nbr = place_ends(jax.random.randint(streams_of[6], (TOP_BLK, TOP_NBR), 0, TOP_BLK), jax.random.fold_in(streams_of[6], 1), 0, TOP_BLK - 1).astype(jnp.int32)
    w_fine_msg = bell_draw(streams_of[7], (WIDTH, WIDTH), WIDTH ** -0.5, 0.375)
    w_fine_self = bell_draw(streams_of[8], (WIDTH, WIDTH), WIDTH ** -0.5, 0.375)
    w_fine_agg = bell_draw(streams_of[9], (WIDTH, WIDTH), WIDTH ** -0.5, 0.375)
    w_fine_out = bell_draw(streams_of[10], (WIDTH, WIDTH), WIDTH ** -0.5, 0.375)
    w_top_msg = bell_draw(streams_of[11], (WIDTH, WIDTH), WIDTH ** -0.5, 0.375)
    w_top_agg = bell_draw(streams_of[12], (WIDTH, WIDTH), WIDTH ** -0.5, 0.375)
    w_down = bell_draw(streams_of[13], (WIDTH, WIDTH), WIDTH ** -0.5, 0.375)
    fine_gain = jnp.clip(1.0 + 0.15 * jax.random.normal(streams_of[14], (WIDTH,), jnp.float32), 0.25, 1.75)
    top_gain = jnp.clip(1.0 + 0.15 * jax.random.normal(streams_of[15], (WIDTH,), jnp.float32), 0.25, 1.75)
    out_gain = jnp.clip(1.0 + 0.15 * jax.random.normal(streams_of[16], (WIDTH,), jnp.float32), 0.25, 1.75)
    return {"fine_state": fine_state, "fine_adj": fine_adj, "fine_nbr": fine_nbr, "up_map": up_map, "up_tiles": up_tiles, "top_adj": top_adj, "top_nbr": top_nbr, "w_fine_msg": w_fine_msg, "w_fine_self": w_fine_self, "w_fine_agg": w_fine_agg, "w_fine_out": w_fine_out, "w_top_msg": w_top_msg, "w_top_agg": w_top_agg, "w_down": w_down, "fine_gain": fine_gain, "top_gain": top_gain, "out_gain": out_gain}


def layer_norm(values, gain):
    center = values - lax.optimization_barrier(jnp.mean(values, -1, keepdims=True))
    spread = lax.optimization_barrier(jnp.mean(center * center, -1, keepdims=True))
    return center * lax.rsqrt(spread + 1e-05) * gain

def reference(fine_state, fine_adj, fine_nbr, up_map, up_tiles, top_adj, top_nbr, w_fine_msg, w_fine_self, w_fine_agg, w_fine_out, w_top_msg, w_top_agg, w_down, fine_gain, top_gain, out_gain):
    f32 = jnp.float32
    bf16 = jnp.bfloat16

    def member_pass(state):
        states = state.astype(f32)
        proj = jnp.einsum('yxnc,cd->yxnd', states, w_fine_msg.astype(f32)).astype(bf16)
        wrapped = jnp.concatenate([proj[:, -1:], proj, proj[:, :1]], axis=1)
        padded = jnp.pad(wrapped, ((1, 1), (0, 0), (0, 0), (0, 0)))
        row_idx = jnp.arange(FINE_Y, dtype=jnp.int32)[:, None, None] + fine_nbr // 3
        col_idx = jnp.arange(FINE_X, dtype=jnp.int32)[None, :, None] + fine_nbr % 3
        picked = padded[row_idx, col_idx]
        agg = jnp.einsum('yxkij,yxkjc->yxic', fine_adj.astype(f32), picked.astype(f32)).astype(bf16)
        inner = jnp.einsum('yxnc,cd->yxnd', states, w_fine_self.astype(f32)) + jnp.einsum('yxnc,cd->yxnd', agg.astype(f32), w_fine_agg.astype(f32))
        hidden = jax.nn.silu(inner).astype(bf16)
        fine_pre = states + jnp.einsum('yxnc,cd->yxnd', hidden.astype(f32), w_fine_out.astype(f32))
        fine_one = layer_norm(fine_pre, fine_gain).astype(bf16)
        contrib = jnp.einsum('yxij,yxjc->yxic', up_tiles.astype(f32), fine_one.astype(f32))
        onehot = (up_map[:, :, None] == jnp.arange(TOP_BLK, dtype=jnp.int32)).astype(f32)
        top_in = jnp.einsum('yxt,yxic->tic', onehot, contrib, precision=lax.Precision.HIGHEST)
        top_zero = layer_norm(top_in, top_gain).astype(bf16)
        tproj = jnp.einsum('tic,cd->tid', top_zero.astype(f32), w_top_msg.astype(f32)).astype(bf16)
        tagg = jnp.einsum('tkij,tkjc->tic', top_adj.astype(f32), tproj[top_nbr].astype(f32)).astype(bf16)
        top_one = (top_zero.astype(f32) + jax.nn.silu(jnp.einsum('tic,cd->tid', tagg.astype(f32), w_top_agg.astype(f32)))).astype(bf16)
        chosen = top_one[up_map]
        down = jnp.einsum('yxji,yxjc->yxic', up_tiles.astype(f32), chosen.astype(f32)).astype(bf16)
        final = fine_one.astype(f32) + jnp.einsum('yxnc,cd->yxnd', down.astype(f32), w_down.astype(f32))
        return layer_norm(final, out_gain).astype(bf16)
    return lax.map(member_pass, fine_state)
```

```python
import functools

import jax
import jax.numpy as jnp
from jax import lax
from jax.experimental import pallas as pl
from jax.experimental.pallas import tpu as pltpu
from jax.sharding import Mesh, PartitionSpec as P

F32 = jnp.float32
BF16 = jnp.bfloat16
VMEM = pl.BlockSpec(memory_space=pltpu.VMEM)
SMEM = pl.BlockSpec(memory_space=pltpu.SMEM)
HBM = pl.BlockSpec(memory_space=pl.ANY)
PARAMS = pltpu.CompilerParams(vmem_limit_bytes=24 * 1024 * 1024)


def dot(a, b):
    return lax.dot_general(a, b, (((1,), (0,)), ((), ())), preferred_element_type=F32)


def dot_t(a, b):
    return lax.dot_general(a, b, (((0,), (0,)), ((), ())), preferred_element_type=F32)


def norm(values, gain):
    center = values - jnp.mean(values, -1, keepdims=True)
    spread = jnp.mean(center * center, -1, keepdims=True)
    return center * lax.rsqrt(spread + 1e-05) * gain


def fine_kernel(
    nbr, up_map, state, up, down, left, right, corner_l, corner_r, adj, tiles,
    w_msg, w_self, w_agg, w_out, gain, fine_out, piece_out, frame,
):
    for c in range(2):
        frame[1 + c] = up[0, 0, c]
        frame[13 + c] = down[0, 0, c]
        for r in range(2):
            frame[(1 + r) * 4 + 1 + c] = state[0, r, c]
    for r in range(2):
        frame[(1 + r) * 4] = left[0, r, 0]
        frame[(1 + r) * 4 + 3] = right[0, r, 0]
        frame[12 * r] = corner_l[r]
        frame[12 * r + 3] = corner_r[r]
    own, mixed = [], []
    for y in range(2):
        for x in range(2):
            picked = []
            for k in range(4):
                code = nbr[y, x, k]
                spot = (y + lax.div(code, 3)) * 4 + x + lax.rem(code, 3)
                picked.append(frame[spot])
            edges = jnp.concatenate([adj[y, x, k] for k in range(4)], axis=1)
            mixed.append(dot(edges, jnp.concatenate(picked, axis=0)).astype(BF16))
            own.append(state[0, y, x])
    own = jnp.concatenate(own, axis=0)
    mixed = jnp.concatenate(mixed, axis=0)
    agg = dot(mixed, w_msg[...]).astype(BF16)
    hidden = jax.nn.silu(dot(own, w_self[...]) + dot(agg, w_agg[...])).astype(BF16)
    fine = norm(own.astype(F32) + dot(hidden, w_out[...]), gain[...]).astype(BF16)
    fine_out[...] = fine
    contrib = [
        dot(tiles[b // 2, b % 2], fine[b * 128 : (b + 1) * 128]).astype(BF16) for b in range(4)
    ]
    contrib = jnp.concatenate(contrib, axis=0)
    row = lax.broadcasted_iota(jnp.int32, (512, 512), 0)
    col = lax.broadcasted_iota(jnp.int32, (512, 512), 1)
    dest = row >> 3
    want = ((row >> 1) & 3) * 128 + (dest & 1) * 64 + (dest >> 1) * 2 + (row & 1)
    order = jnp.where(col == want, 1.0, 0.0).astype(BF16)
    piece = dot(order, contrib).reshape(64, 8, 256)
    line = lax.broadcasted_iota(jnp.int32, (64, 8, 256), 1) >> 1
    label = jnp.where(
        line < 2,
        jnp.where(line == 0, up_map[0, 0], up_map[0, 1]),
        jnp.where(line == 2, up_map[1, 0], up_map[1, 1]),
    ).astype(F32)
    piece_out[...] = jnp.concatenate([piece, label], axis=1).astype(BF16)


def sum_kernel(got, gain, share_out):
    wide = got[...].astype(F32)
    values = wide[:, :8, :].reshape(512, 256).astype(BF16)
    label = wide[:, 8:, :128].reshape(512, 128).astype(jnp.int32)
    row = lax.broadcasted_iota(jnp.int32, (512, 128), 0)
    col = lax.broadcasted_iota(jnp.int32, (512, 128), 1)
    member = jnp.where((label * 2 + (row & 1)) == col, 1.0, 0.0).astype(BF16)
    total = dot_t(member, values)[:40]
    share = norm(total, gain[...]).astype(BF16)
    share_out[...] = jnp.broadcast_to(share[None], share_out.shape)


def top_kernel(
    up_map, top_nbr, mine, other, fine, tiles, w_msg, w_agg, w_down, gain, top_adj,
    out, top, adj, sems, *, core_axis,
):
    copies = []
    for b in range(4):
        copy = pltpu.make_async_copy(top_adj.at[up_map[b // 2, b % 2]], adj.at[b], sems.at[b])
        copy.start()
        copies.append(copy)
    core = lax.axis_index(core_axis)
    row = lax.broadcasted_iota(jnp.int32, (320, 320), 0)
    col = lax.broadcasted_iota(jnp.int32, (320, 320), 1)
    want = ((row & 15) >> 1) * 40 + (row >> 4) * 2 + (row & 1)
    order = jnp.where(col == want, 1.0, 0.0).astype(BF16)
    for source, half in ((mine, core), (other, 1 - core)):
        for g in range(4):
            block = source[8 * g : 8 * g + 8].reshape(320, 256)
            moved = dot(order, block).astype(BF16).reshape(20, 16, 256)
            start = pl.multiple_of(half * 64 + g * 16, 16)
            top[:, pl.ds(start, 16), :] = moved
    mixed, chosen = [], []
    for b in range(4):
        at = up_map[b // 2, b % 2]
        chosen.append(top[at])
        picked = jnp.concatenate([top[top_nbr[at, k]] for k in range(4)], axis=0)
        copies[b].wait()
        edges = jnp.concatenate([adj[b, k] for k in range(4)], axis=1)
        mixed.append(dot(edges, picked).astype(BF16))
    chosen = jnp.concatenate(chosen, axis=0)
    mixed = jnp.concatenate(mixed, axis=0)
    tagg = dot(mixed, w_msg[...]).astype(BF16)
    one = (chosen.astype(F32) + jax.nn.silu(dot(tagg, w_agg[...]))).astype(BF16)
    lower = [
        dot_t(tiles[b // 2, b % 2], one[b * 128 : (b + 1) * 128]).astype(BF16) for b in range(4)
    ]
    lower = jnp.concatenate(lower, axis=0)
    final = norm(fine[...].astype(F32) + dot(lower, w_down[...]), gain[...]).astype(BF16)
    out[...] = final.reshape(1, 2, 2, 128, 256)


def local(
    fine_state, fine_adj, fine_nbr, up_map, up_tiles, top_adj, top_nbr, w_fine_msg, w_fine_self,
    w_fine_agg, w_fine_out, w_top_msg, w_top_agg, w_down, fine_gain, top_gain, out_gain,
):
    sx = ("x", "core")
    rows, cols = lax.axis_size("sy"), lax.axis_size("x") * lax.axis_size("core")
    east = [(i, (i + 1) % cols) for i in range(cols)]
    west = [(j, i) for i, j in east]
    south = [(i, i + 1) for i in range(rows - 1)]
    north = [(j, i) for i, j in south]
    up = lax.ppermute(fine_state[:, 1:2], "sy", south)
    down = lax.ppermute(fine_state[:, 0:1], "sy", north)
    left = lax.ppermute(fine_state[:, :, 1:2], sx, east)
    right = lax.ppermute(fine_state[:, :, 0:1], sx, west)
    corner_l = lax.ppermute(jnp.concatenate([up[0, :, 1], down[0, :, 1]]), sx, east)
    corner_r = lax.ppermute(jnp.concatenate([up[0, :, 0], down[0, :, 0]]), sx, west)
    fine, piece = pl.pallas_call(
        fine_kernel,
        out_shape=(
            jax.ShapeDtypeStruct((512, 256), BF16),
            jax.ShapeDtypeStruct((64, 16, 256), BF16),
        ),
        in_specs=[SMEM, SMEM] + [VMEM] * 14,
        out_specs=(VMEM, VMEM),
        scratch_shapes=[pltpu.VMEM((16, 128, 256), BF16)],
        compiler_params=PARAMS,
        name="fine_level",
    )(
        fine_nbr, up_map, fine_state, up, down, left, right, corner_l, corner_r, fine_adj,
        up_tiles, w_fine_msg, w_fine_self, w_fine_agg, w_fine_out, fine_gain[None],
    )
    got = lax.all_to_all(piece, ("sy", "x", "core"), 0, 0)
    share = pl.pallas_call(
        sum_kernel,
        out_shape=jax.ShapeDtypeStruct((32, 40, 256), BF16),
        in_specs=[VMEM] * 2,
        out_specs=VMEM,
        compiler_params=PARAMS,
        name="top_sum",
    )(got, top_gain[None])
    mine = lax.all_to_all(share, ("sy", "x"), 0, 0)
    other = lax.ppermute(mine, "core", [(0, 1), (1, 0)])
    return pl.pallas_call(
        functools.partial(top_kernel, core_axis="core"),
        out_shape=jax.ShapeDtypeStruct(fine_state.shape, BF16),
        in_specs=[SMEM, SMEM] + [VMEM] * 8 + [HBM],
        out_specs=VMEM,
        scratch_shapes=[
            pltpu.VMEM((20, 128, 256), BF16),
            pltpu.VMEM((4, 4, 128, 128), BF16),
            pltpu.SemaphoreType.DMA((4,)),
        ],
        compiler_params=PARAMS,
        name="top_level",
    )(
        up_map, top_nbr, mine, other, fine, up_tiles, w_top_msg, w_top_agg, w_down,
        out_gain[None], top_adj,
    )


def solution(mesh):
    shape = dict(mesh.shape)
    inner = Mesh(
        mesh.devices.reshape(shape["ens"], shape["sy"], shape["sx"] // 2, 2),
        ("ens", "sy", "x", "core"),
    )
    sx = ("x", "core")
    in_specs = (
        P("ens", "sy", sx, None, None),
        P("sy", sx, None, None, None),
        P("sy", sx, None),
        P("sy", sx),
        P("sy", sx, None, None),
    ) + (P(),) * 12
    out_specs = P("ens", "sy", sx, None, None)
    return jax.shard_map(local, mesh=inner, in_specs=in_specs, out_specs=out_specs, check_vma=False)
```

```python
import functools

import jax
import jax.numpy as jnp
from jax import lax
from jax.experimental import pallas as pl
from jax.experimental.pallas import tpu as pltpu
from jax.sharding import Mesh, PartitionSpec as P

F32 = jnp.float32
BF16 = jnp.bfloat16
VMEM = pl.BlockSpec(memory_space=pltpu.VMEM)
HBM = pl.BlockSpec(memory_space=pltpu.HBM)
MIB = 1024 * 1024


def dot(a, b):
    return lax.dot_general(a, b, (((1,), (0,)), ((), ())), preferred_element_type=F32)


def dot_t(a, b):
    return lax.dot_general(a, b, (((0,), (0,)), ((), ())), preferred_element_type=F32)


def norm(values, gain):
    center = values - jnp.mean(values, -1, keepdims=True)
    spread = jnp.mean(center * center, -1, keepdims=True)
    return center * lax.rsqrt(spread + 1e-05) * gain


def far(array):
    return pltpu.with_memory_space_constraint(array, pltpu.HBM)


def start_all(pairs, sems):
    copies = [pltpu.make_async_copy(src, dst, sems.at[n]) for n, (src, dst) in enumerate(pairs)]
    for copy in copies:
        copy.start()
    return copies


def cut_kernel(state, last_row, first_row, last_col, first_col, sems):
    pairs = [
        (state.at[:, 1:2], last_row),
        (state.at[:, 0:1], first_row),
        (state.at[:, :, 1:2], last_col),
        (state.at[:, :, 0:1], first_col),
    ]
    for copy in start_all(pairs, sems):
        copy.wait()


def stage_kernel(
    state_in, w_self_in, nbr_in, map_in, adj_in, tiles_in, w_msg_in, w_agg_in, w_out_in, gain_in,
    state, own_part, nbr, up_map, adj, tiles, w_msg, w_agg, w_out, gain, w_self, sems,
):
    pairs = [
        (state_in, state), (w_self_in, w_self), (nbr_in, nbr), (map_in, up_map), (adj_in, adj),
        (tiles_in, tiles), (w_msg_in, w_msg), (w_agg_in, w_agg), (w_out_in, w_out),
        (gain_in, gain),
    ]
    copies = start_all(pairs, sems)
    copies[0].wait()
    copies[1].wait()
    own = jnp.concatenate([state[0, b // 2, b % 2] for b in range(4)], axis=0)
    own_part[...] = dot(own, w_self[...])
    for copy in copies[2:]:
        copy.wait()


def fine_kernel(
    up, down, left, right, corner_l, corner_r, state, own_part, nbr_in, map_in, adj, tiles,
    w_msg, w_agg, w_out, gain, fine_out, piece_out, frame, nbr, up_map, sems,
):
    copies = start_all([(nbr_in, nbr), (map_in, up_map)], sems)
    for c in range(2):
        frame[1 + c] = up[0, 0, c]
        frame[13 + c] = down[0, 0, c]
        for r in range(2):
            frame[(1 + r) * 4 + 1 + c] = state[0, r, c]
    for r in range(2):
        frame[(1 + r) * 4] = left[0, r, 0]
        frame[(1 + r) * 4 + 3] = right[0, r, 0]
        frame[12 * r] = corner_l[r]
        frame[12 * r + 3] = corner_r[r]
    for copy in copies:
        copy.wait()
    own, mixed = [], []
    for y in range(2):
        for x in range(2):
            picked = []
            for k in range(4):
                code = nbr[y, x, k]
                spot = (y + lax.div(code, 3)) * 4 + x + lax.rem(code, 3)
                picked.append(frame[spot])
            edges = jnp.concatenate([adj[y, x, k] for k in range(4)], axis=1)
            mixed.append(dot(edges, jnp.concatenate(picked, axis=0)).astype(BF16))
            own.append(frame[(1 + y) * 4 + 1 + x])
    own = jnp.concatenate(own, axis=0)
    mixed = jnp.concatenate(mixed, axis=0)
    agg = dot(mixed, w_msg[...]).astype(BF16)
    hidden = jax.nn.silu(own_part[...] + dot(agg, w_agg[...])).astype(BF16)
    fine = norm(own.astype(F32) + dot(hidden, w_out[...]), gain[...]).astype(BF16)
    fine_out[...] = fine
    contrib = [
        dot(tiles[b // 2, b % 2], fine[b * 128 : (b + 1) * 128]).astype(BF16) for b in range(4)
    ]
    row = lax.broadcasted_iota(jnp.int32, (128, 128), 0)
    col = lax.broadcasted_iota(jnp.int32, (128, 128), 1)
    dest = row >> 3
    want = ((row >> 1) & 3) * 32 + (dest & 1) * 16 + (dest >> 1) * 2 + (row & 1)
    order = jnp.where(col == want, 1.0, 0.0).astype(BF16)
    piece = []
    for g in range(4):
        spots = [(b, 64 * core + 16 * g) for b in range(4) for core in range(2)]
        rows = jnp.concatenate([contrib[b][at : at + 16] for b, at in spots], axis=0)
        piece.append(dot(order, rows))
    piece = jnp.concatenate(piece, axis=0).reshape(64, 8, 256)
    line = lax.broadcasted_iota(jnp.int32, (64, 8, 128), 1) >> 1
    label = jnp.where(
        line < 2,
        jnp.where(line == 0, up_map[0, 0], up_map[0, 1]),
        jnp.where(line == 2, up_map[1, 0], up_map[1, 1]),
    ).astype(F32)
    parts = [piece[:, :, :128], piece[:, :, 128:], label]
    piece_out[...] = jnp.concatenate(parts, axis=1).astype(BF16)


def sum_kernel(got, gain, share_out):
    wide = got[...].astype(F32)
    values = jnp.concatenate([wide[:, :8], wide[:, 8:16]], axis=2).reshape(512, 256).astype(BF16)
    label = wide[:, 16:].reshape(512, 128).astype(jnp.int32)
    row = lax.broadcasted_iota(jnp.int32, (512, 128), 0)
    col = lax.broadcasted_iota(jnp.int32, (512, 128), 1)
    member = jnp.where((label * 2 + (row & 1)) == col, 1.0, 0.0).astype(BF16)
    total = dot_t(member, values)[:40]
    share = norm(total, gain[...]).astype(BF16)
    share_out[...] = jnp.broadcast_to(share[None], share_out.shape)


def spread_rows(source, top):
    row = lax.broadcasted_iota(jnp.int32, (160, 160), 0)
    col = lax.broadcasted_iota(jnp.int32, (160, 160), 1)
    want = ((row & 7) >> 1) * 40 + (row >> 3) * 2 + (row & 1)
    order = jnp.where(col == want, 1.0, 0.0).astype(BF16)
    for g in range(4):
        moved = [
            dot(order, source[8 * g + 4 * h : 8 * g + 4 * h + 4].reshape(160, 256))
            for h in range(2)
        ]
        moved = jnp.concatenate([part.reshape(20, 8, 256) for part in moved], axis=1)
        top[:, 16 * g : 16 * g + 16, :] = moved.astype(BF16)


def gather_parts(up_map, top_nbr, edges, top):
    mixed = []
    for b in range(4):
        at = up_map[b // 2, b % 2]
        picked = jnp.concatenate([top[top_nbr[k, at]] for k in range(4)], axis=0)
        mixed.append(dot(edges[b], picked))
    return jnp.concatenate(mixed, axis=0)


def half_kernel(
    map_in, nbr_in, mine, adj_in, fine_in, tiles_in, w_msg_in, w_agg_in, w_down_in, gain_in,
    edges, mixed, chosen, fine, tiles, w_msg, w_agg, w_down, gain,
    top, near, adj, up_map, top_nbr, sems, *, core_axis,
):
    first = start_all([(map_in, up_map), (nbr_in, top_nbr)], sems)
    rest = [
        (fine_in, fine), (tiles_in, tiles), (w_msg_in, w_msg), (w_agg_in, w_agg),
        (w_down_in, w_down), (gain_in, gain),
    ]
    rest = start_all(rest, sems.at[pl.ds(6, 6)])
    for copy in first:
        copy.wait()
    pairs = [(adj_in.at[up_map[b // 2, b % 2]], adj.at[b]) for b in range(4)]
    copies = start_all(pairs, sems.at[pl.ds(2, 4)])
    spread_rows(mine, top)
    core = lax.axis_index(core_axis)
    for b in range(4):
        copies[b].wait()
        low = jnp.concatenate([adj[b, k][:, :64] for k in range(4)], axis=1)
        high = jnp.concatenate([adj[b, k][:, 64:] for k in range(4)], axis=1)
        near[b] = jnp.where(core == 0, low, high)
        edges[b] = jnp.where(core == 0, high, low)
        chosen[b] = top[up_map[b // 2, b % 2]]
    mixed[...] = gather_parts(up_map, top_nbr, near, top)
    for copy in rest:
        copy.wait()


def top_kernel(
    map_in, nbr_in, other, edges, mixed, chosen, fine, tiles, w_msg, w_agg, w_down, gain,
    out, top, whole, up_map, top_nbr, sems, *, core_axis,
):
    copies = start_all([(map_in, up_map), (nbr_in, top_nbr)], sems)
    spread_rows(other, top)
    for copy in copies:
        copy.wait()
    core = lax.axis_index(core_axis)
    here = pl.ds(pl.multiple_of(core * 64, 64), 64)
    there = pl.ds(pl.multiple_of((1 - core) * 64, 64), 64)
    for b in range(4):
        whole[b, here, :] = chosen[b]
        whole[b, there, :] = top[up_map[b // 2, b % 2]]
    both = mixed[...] + gather_parts(up_map, top_nbr, edges, top)
    tagg = dot(both.astype(BF16), w_msg[...]).astype(BF16)
    zero = jnp.concatenate([whole[b] for b in range(4)], axis=0).astype(F32)
    one = (zero + jax.nn.silu(dot(tagg, w_agg[...]))).astype(BF16)
    lower = [
        dot_t(tiles[b // 2, b % 2], one[b * 128 : (b + 1) * 128]).astype(BF16) for b in range(4)
    ]
    lower = jnp.concatenate(lower, axis=0)
    final = norm(fine[...].astype(F32) + dot(lower, w_down[...]), gain[...]).astype(BF16)
    out[...] = final.reshape(1, 2, 2, 128, 256)


def call(body, ins, outs, scratch, name, busy=0, limit=24):
    return pl.pallas_call(
        body,
        out_shape=tuple(jax.ShapeDtypeStruct(shape, kind) for shape, kind in outs),
        in_specs=ins,
        out_specs=(VMEM,) * len(outs),
        scratch_shapes=scratch,
        compiler_params=pltpu.CompilerParams(vmem_limit_bytes=limit * MIB),
        cost_estimate=pl.CostEstimate(flops=0, bytes_accessed=busy, transcendentals=0),
        name=name,
    )


def local(
    fine_state, fine_adj, fine_nbr, up_map, up_tiles, top_adj, top_nbr, w_fine_msg, w_fine_self,
    w_fine_agg, w_fine_out, w_top_msg, w_top_agg, w_down, fine_gain, top_gain, out_gain,
):
    sx = ("x", "core")
    rows, cols = lax.axis_size("sy"), lax.axis_size("x") * lax.axis_size("core")
    east = [(i, (i + 1) % cols) for i in range(cols)]
    west = [(j, i) for i, j in east]
    south = [(i, i + 1) for i in range(rows - 1)]
    north = [(j, i) for i, j in south]
    weight = ((256, 256), BF16)
    tile_set = ((2, 2, 128, 128), BF16)
    part = ((512, 256), F32)
    gain = ((1, 256), F32)
    row_cut, col_cut = ((1, 1, 2, 128, 256), BF16), ((1, 2, 1, 128, 256), BF16)
    dma = pltpu.SemaphoreType.DMA
    last_row, first_row, last_col, first_col = call(
        cut_kernel, [HBM], [row_cut, row_cut, col_cut, col_cut], [dma((4,))], "cut", 1 << 20
    )(far(fine_state))
    up = lax.ppermute(last_row, "sy", south)
    down = lax.ppermute(first_row, "sy", north)
    left = lax.ppermute(last_col, sx, east)
    right = lax.ppermute(first_col, sx, west)
    corner_l = lax.ppermute(jnp.concatenate([up[0, :, 1], down[0, :, 1]]), sx, east)
    corner_r = lax.ppermute(jnp.concatenate([up[0, :, 0], down[0, :, 0]]), sx, west)
    staged = [
        fine_nbr, up_map, fine_adj, up_tiles, w_fine_msg, w_fine_agg, w_fine_out, fine_gain[None],
    ]
    held = call(
        stage_kernel,
        [HBM] * 10,
        [(fine_state.shape, BF16), part] + [(array.shape, array.dtype) for array in staged],
        [pltpu.VMEM(*weight), dma((10,))],
        "stage",
        1 << 23,
    )(*[far(array) for array in [fine_state, w_fine_self] + staged])
    fine, piece = call(
        fine_kernel,
        [VMEM] * 16,
        [((512, 256), BF16), ((64, 24, 128), BF16)],
        [
            pltpu.VMEM((16, 128, 256), BF16), pltpu.SMEM((2, 2, 4), jnp.int32),
            pltpu.SMEM((2, 2), jnp.int32), dma((2,)),
        ],
        "fine_level",
        1 << 23,
    )(up, down, left, right, corner_l, corner_r, *held)
    got = lax.all_to_all(piece, ("sy", "x", "core"), 0, 0)
    (share,) = call(
        sum_kernel, [VMEM] * 2, [((32, 40, 256), BF16)], [], "top_sum", 1 << 20
    )(got, top_gain[None])
    mine = lax.all_to_all(share, ("sy", "x"), 0, 0)
    other = lax.ppermute(mine, "core", [(0, 1), (1, 0)])
    tables = [pltpu.SMEM((2, 2), jnp.int32), pltpu.SMEM((4, 20), jnp.int32)]
    top = pltpu.VMEM((20, 64, 256), BF16)
    half_set = ((4, 128, 256), BF16)
    half = call(
        functools.partial(half_kernel, core_axis="core"),
        [HBM] * 2 + [VMEM] + [HBM] * 7,
        [
            half_set, part, ((4, 64, 256), BF16), ((512, 256), BF16), tile_set, weight, weight, weight, gain,
        ],
        [top, pltpu.VMEM(*half_set), pltpu.VMEM((4, 4, 128, 128), BF16)] + tables + [dma((12,))],
        "top_half",
        1 << 23,
    )(
        up_map, top_nbr.T, mine, top_adj, fine, up_tiles, w_top_msg, w_top_agg, w_down,
        out_gain[None],
    )
    (out,) = call(
        functools.partial(top_kernel, core_axis="core"),
        [HBM] * 2 + [VMEM] * 10,
        [(fine_state.shape, BF16)],
        [top, pltpu.VMEM(*half_set)] + tables + [dma((2,))],
        "top_level",
        1 << 23,
    )(up_map, top_nbr.T, other, *half)
    return out


def solution(mesh):
    shape = dict(mesh.shape)
    inner = Mesh(
        mesh.devices.reshape(shape["ens"], shape["sy"], shape["sx"] // 2, 2),
        ("ens", "sy", "x", "core"),
    )
    sx = ("x", "core")
    in_specs = (
        P("ens", "sy", sx, None, None),
        P("sy", sx, None, None, None),
        P("sy", sx, None),
        P("sy", sx),
        P("sy", sx, None, None),
    ) + (P(),) * 12
    out_specs = P("ens", "sy", sx, None, None)
    return jax.shard_map(local, mesh=inner, in_specs=in_specs, out_specs=out_specs, check_vma=False)
```

```python
import functools

import jax
import jax.numpy as jnp
from jax import lax
from jax.experimental import pallas as pl
from jax.experimental.pallas import tpu as pltpu
from jax.sharding import Mesh, PartitionSpec as P

F32 = jnp.float32
BF16 = jnp.bfloat16
VMEM = pl.BlockSpec(memory_space=pltpu.VMEM)
HBM = pl.BlockSpec(memory_space=pltpu.HBM)
MIB = 1024 * 1024


def dot(a, b):
    return lax.dot_general(a, b, (((1,), (0,)), ((), ())), preferred_element_type=F32)


def dot_t(a, b):
    return lax.dot_general(a, b, (((0,), (0,)), ((), ())), preferred_element_type=F32)


def norm(values, gain):
    center = values - jnp.mean(values, -1, keepdims=True)
    spread = jnp.mean(center * center, -1, keepdims=True)
    return center * lax.rsqrt(spread + 1e-05) * gain


def far(array):
    return pltpu.with_memory_space_constraint(array, pltpu.HBM)


def start_all(pairs, sems):
    copies = [pltpu.make_async_copy(src, dst, sems.at[n]) for n, (src, dst) in enumerate(pairs)]
    for copy in copies:
        copy.start()
    return copies


def cut_kernel(state, last_row, first_row, last_col, first_col, sems):
    pairs = [
        (state.at[:, 1:2], last_row),
        (state.at[:, 0:1], first_row),
        (state.at[:, :, 1:2], last_col),
        (state.at[:, :, 0:1], first_col),
    ]
    for copy in start_all(pairs, sems):
        copy.wait()


def stage_kernel(
    state_in, w_self_in, map_in, nbr_in, adj_in, tiles_in, w_msg_in, w_agg_in, w_out_in, gain_in,
    top_adj, state, own_part, up_map, nbr, adj, tiles, w_msg, w_agg, w_out, gain,
    turned, near, away, w_self, table, edges, sems, *, core_axis,
):
    first = pltpu.make_async_copy(map_in, table, sems.at[10])
    first.start()
    pairs = [
        (state_in, state), (w_self_in, w_self), (map_in, up_map), (nbr_in, nbr), (adj_in, adj),
        (tiles_in, tiles), (w_msg_in, w_msg), (w_agg_in, w_agg), (w_out_in, w_out),
        (gain_in, gain),
    ]
    copies = start_all(pairs, sems)
    first.wait()
    pairs = [(top_adj.at[table[b // 2, b % 2]], edges.at[b]) for b in range(4)]
    edge_copies = start_all(pairs, sems.at[pl.ds(11, 4)])
    copies[0].wait()
    copies[1].wait()
    own = jnp.concatenate([state[0, b // 2, b % 2] for b in range(4)], axis=0)
    own_part[...] = dot(own, w_self[...])
    for copy in copies[2:]:
        copy.wait()
    core = lax.axis_index(core_axis)
    for b in range(4):
        turned[b // 2, b % 2] = tiles[b // 2, b % 2].T
        edge_copies[b].wait()
        low = jnp.concatenate([edges[b, k][:, :64] for k in range(4)], axis=1)
        high = jnp.concatenate([edges[b, k][:, 64:] for k in range(4)], axis=1)
        near[b] = jnp.where(core == 0, low, high)
        away[b] = jnp.where(core == 0, high, low)


def fine_kernel(
    up, down, left, right, corner_l, corner_r, state, own_part, map_in, nbr_in, adj, tiles,
    w_msg, w_agg, w_out, gain, fine_out, piece_out, frame, nbr, up_map, sems,
):
    copies = start_all([(nbr_in, nbr), (map_in, up_map)], sems)
    for c in range(2):
        frame[1 + c] = up[0, 0, c]
        frame[13 + c] = down[0, 0, c]
        for r in range(2):
            frame[(1 + r) * 4 + 1 + c] = state[0, r, c]
    for r in range(2):
        frame[(1 + r) * 4] = left[0, r, 0]
        frame[(1 + r) * 4 + 3] = right[0, r, 0]
        frame[12 - 12 * r] = corner_l[r]
        frame[15 - 12 * r] = corner_r[r]
    for copy in copies:
        copy.wait()
    own, mixed = [], []
    for y in range(2):
        for x in range(2):
            picked = []
            for k in range(4):
                code = nbr[y, x, k]
                spot = (y + lax.div(code, 3)) * 4 + x + lax.rem(code, 3)
                picked.append(frame[spot])
            edges = jnp.concatenate([adj[y, x, k] for k in range(4)], axis=1)
            mixed.append(dot(edges, jnp.concatenate(picked, axis=0)).astype(BF16))
            own.append(frame[(1 + y) * 4 + 1 + x])
    own = jnp.concatenate(own, axis=0)
    mixed = jnp.concatenate(mixed, axis=0)
    agg = dot(mixed, w_msg[...]).astype(BF16)
    hidden = jax.nn.silu(own_part[...] + dot(agg, w_agg[...])).astype(BF16)
    fine = norm(own.astype(F32) + dot(hidden, w_out[...]), gain[...]).astype(BF16)
    fine_out[...] = fine
    contrib = [
        dot(tiles[b // 2, b % 2], fine[b * 128 : (b + 1) * 128]).astype(BF16) for b in range(4)
    ]
    row = lax.broadcasted_iota(jnp.int32, (128, 128), 0)
    col = lax.broadcasted_iota(jnp.int32, (128, 128), 1)
    dest = row >> 3
    want = ((row >> 1) & 3) * 32 + (dest & 1) * 16 + (dest >> 1) * 2 + (row & 1)
    order = jnp.where(col == want, 1.0, 0.0).astype(BF16)
    piece = []
    for g in range(4):
        spots = [(b, 64 * core + 16 * g) for b in range(4) for core in range(2)]
        rows = jnp.concatenate([contrib[b][at : at + 16] for b, at in spots], axis=0)
        piece.append(dot(order, rows))
    piece = jnp.concatenate(piece, axis=0).reshape(64, 8, 256)
    line = lax.broadcasted_iota(jnp.int32, (64, 8, 128), 1) >> 1
    label = jnp.where(
        line < 2,
        jnp.where(line == 0, up_map[0, 0], up_map[0, 1]),
        jnp.where(line == 2, up_map[1, 0], up_map[1, 1]),
    ).astype(F32)
    parts = [piece[:, :, :128], piece[:, :, 128:], label]
    piece_out[...] = jnp.concatenate(parts, axis=1).astype(BF16)


def sum_kernel(got, gain, share_out):
    wide = got[...].astype(F32)
    values = jnp.concatenate([wide[:, :8], wide[:, 8:16]], axis=2).reshape(512, 256).astype(BF16)
    label = wide[:, 16:].reshape(512, 128).astype(jnp.int32)
    row = lax.broadcasted_iota(jnp.int32, (512, 128), 0)
    col = lax.broadcasted_iota(jnp.int32, (512, 128), 1)
    member = jnp.where((label * 2 + (row & 1)) == col, 1.0, 0.0).astype(BF16)
    total = dot_t(member, values)[:40]
    share = norm(total, gain[...]).astype(BF16)
    share_out[...] = jnp.broadcast_to(share[None], share_out.shape)


def order_kernel(got, out):
    row = lax.broadcasted_iota(jnp.int32, (160, 160), 0)
    col = lax.broadcasted_iota(jnp.int32, (160, 160), 1)
    want = ((row & 7) >> 1) * 40 + (row >> 3) * 2 + (row & 1)
    order = jnp.where(col == want, 1.0, 0.0).astype(BF16)
    moved = [dot(order, got[4 * h : 4 * h + 4].reshape(160, 256)) for h in range(2)]
    moved = jnp.concatenate([part.reshape(20, 8, 256) for part in moved], axis=1)
    out[...] = jnp.broadcast_to(moved.astype(BF16)[None], out.shape)


def half_block(source, at):
    return jnp.concatenate([source[x, at] for x in range(4)], axis=0)


def gather_parts(up_map, top_nbr, edges, source):
    mixed = []
    for b in range(4):
        at = up_map[b // 2, b % 2]
        picked = jnp.concatenate([half_block(source, top_nbr[k, at]) for k in range(4)], axis=0)
        mixed.append(dot(edges[b], picked))
    return jnp.concatenate(mixed, axis=0)


def half_kernel(map_in, nbr_in, mine, near, mixed, chosen, up_map, top_nbr, sems):
    for copy in start_all([(map_in, up_map), (nbr_in, top_nbr)], sems):
        copy.wait()
    for b in range(4):
        chosen[b] = half_block(mine, up_map[b // 2, b % 2])
    mixed[...] = gather_parts(up_map, top_nbr, near, mine)


def top_kernel(
    map_in, nbr_in, other, away, mixed, chosen, fine, turned, w_msg, w_agg, w_down, gain,
    out, whole, up_map, top_nbr, sems, *, core_axis,
):
    copies = start_all([(map_in, up_map), (nbr_in, top_nbr)], sems)
    core = lax.axis_index(core_axis)
    here = pl.ds(pl.multiple_of(core * 64, 64), 64)
    there = pl.ds(pl.multiple_of((1 - core) * 64, 64), 64)
    for b in range(4):
        whole[b, here, :] = chosen[b]
    for copy in copies:
        copy.wait()
    for b in range(4):
        whole[b, there, :] = half_block(other, up_map[b // 2, b % 2])
    both = mixed[...] + gather_parts(up_map, top_nbr, away, other)
    tagg = dot(both.astype(BF16), w_msg[...]).astype(BF16)
    zero = jnp.concatenate([whole[b] for b in range(4)], axis=0).astype(F32)
    one = (zero + jax.nn.silu(dot(tagg, w_agg[...]))).astype(BF16)
    copies = []
    for b in range(4):
        rows = slice(b * 128, (b + 1) * 128)
        lower = dot(turned[b // 2, b % 2], one[rows]).astype(BF16)
        final = norm(fine[rows].astype(F32) + dot(lower, w_down[...]), gain[...])
        whole[b] = final.astype(BF16)
        copy = pltpu.make_async_copy(whole.at[b], out.at[0, b // 2, b % 2], sems.at[2 + b])
        copy.start()
        copies.append(copy)
    for copy in copies:
        copy.wait()


def call(body, ins, outs, scratch, name, busy=0, limit=24, place=VMEM):
    return pl.pallas_call(
        body,
        out_shape=tuple(jax.ShapeDtypeStruct(shape, kind) for shape, kind in outs),
        in_specs=ins,
        out_specs=(place,) * len(outs),
        scratch_shapes=scratch,
        compiler_params=pltpu.CompilerParams(vmem_limit_bytes=limit * MIB),
        cost_estimate=pl.CostEstimate(flops=0, bytes_accessed=busy, transcendentals=0),
        name=name,
    )


def local(
    fine_state, fine_adj, fine_nbr, up_map, up_tiles, top_adj, top_nbr, w_fine_msg, w_fine_self,
    w_fine_agg, w_fine_out, w_top_msg, w_top_agg, w_down, fine_gain, top_gain, out_gain,
):
    sx = ("x", "core")
    rows, cols = lax.axis_size("sy"), lax.axis_size("x") * lax.axis_size("core")
    east = [(i, (i + 1) % cols) for i in range(cols)]
    west = [(j, i) for i, j in east]
    twin = [(0, 1), (1, 0)]
    south = [(i, i + 1) for i in range(rows - 1)]
    north = [(j, i) for i, j in south]
    weight = ((256, 256), BF16)
    tile_set = ((2, 2, 128, 128), BF16)
    part = ((512, 256), F32)
    gain = ((1, 256), F32)
    row_cut, col_cut = ((1, 1, 2, 128, 256), BF16), ((1, 2, 1, 128, 256), BF16)
    dma = pltpu.SemaphoreType.DMA
    last_row, first_row, last_col, first_col = call(
        cut_kernel, [HBM], [row_cut, row_cut, col_cut, col_cut], [dma((4,))], "cut", 1 << 20
    )(far(fine_state))
    down = lax.ppermute(first_row, "sy", north)
    up = lax.ppermute(last_row, "sy", south)
    left = lax.ppermute(last_col, sx, east)
    right = lax.ppermute(first_col, sx, west)
    half_set = ((4, 128, 256), BF16)
    staged = [
        up_map, fine_nbr, fine_adj, up_tiles, w_fine_msg, w_fine_agg, w_fine_out, fine_gain[None],
    ]
    *held, turned, near, away = call(
        functools.partial(stage_kernel, core_axis="core"),
        [HBM] * 11,
        [(fine_state.shape, BF16), part]
        + [(array.shape, array.dtype) for array in staged]
        + [tile_set, half_set, half_set],
        [
            pltpu.VMEM(*weight), pltpu.SMEM((2, 2), jnp.int32),
            pltpu.VMEM((4, 4, 128, 128), BF16), dma((15,)),
        ],
        "stage",
        1 << 23,
    )(*[far(array) for array in [fine_state, w_fine_self] + staged + [top_adj]])
    down, up, held = lax.optimization_barrier((down, up, held))
    corner_l = lax.ppermute(jnp.concatenate([down[0, :, 1], up[0, :, 1]]), sx, east)
    corner_r = lax.ppermute(jnp.concatenate([down[0, :, 0], up[0, :, 0]]), sx, west)
    fine, piece = call(
        fine_kernel,
        [VMEM] * 16,
        [((512, 256), BF16), ((64, 24, 128), BF16)],
        [
            pltpu.VMEM((16, 128, 256), BF16), pltpu.SMEM((2, 2, 4), jnp.int32),
            pltpu.SMEM((2, 2), jnp.int32), dma((2,)),
        ],
        "fine_level",
        1 << 23,
    )(up, down, left, right, corner_l, corner_r, *held)
    chips = lax.axis_size("x") * rows
    back = [2 * chip + core for chip in range(chips - 1, -1, -1) for core in range(2)]
    got = lax.all_to_all(piece, ("x", "sy", "core"), 0, 0, axis_index_groups=[back])
    (share,) = call(
        sum_kernel, [VMEM] * 2, [((8, 40, 256), BF16)], [], "top_sum", 1 << 20
    )(got, top_gain[None])
    column = lax.all_to_all(share, "sy", 0, 0, axis_index_groups=[list(range(rows - 1, -1, -1))])
    (column,) = call(
        order_kernel, [VMEM], [((4, 20, 16, 256), BF16)], [], "top_order", 1 << 20
    )(column)
    mine = lax.all_to_all(column, "x", 0, 0, axis_index_groups=[list(range(cols // 2 - 1, -1, -1))])
    other = lax.ppermute(mine, "core", twin)
    tables = [pltpu.SMEM((2, 2), jnp.int32), pltpu.SMEM((4, 20), jnp.int32)]
    mixed, chosen = call(
        half_kernel,
        [HBM] * 2 + [VMEM] * 2,
        [part, ((4, 64, 256), BF16)],
        tables + [dma((2,))],
        "top_half",
        1 << 23,
    )(up_map, top_nbr.T, mine, near)
    (out,) = call(
        functools.partial(top_kernel, core_axis="core"),
        [HBM] * 2 + [VMEM] * 10,
        [(fine_state.shape, BF16)],
        [pltpu.VMEM(*half_set)] + tables + [dma((6,))],
        "top_level",
        1 << 23,
        place=HBM,
    )(
        up_map, top_nbr.T, other, away, mixed, chosen, fine, turned, w_top_msg, w_top_agg,
        w_down, out_gain[None],
    )
    return out


def solution(mesh):
    shape = dict(mesh.shape)
    inner = Mesh(
        mesh.devices.reshape(shape["ens"], shape["sy"], shape["sx"] // 2, 2),
        ("ens", "sy", "x", "core"),
    )
    sx = ("x", "core")
    in_specs = (
        P("ens", "sy", sx, None, None),
        P("sy", sx, None, None, None),
        P("sy", sx, None),
        P("sy", sx),
        P("sy", sx, None, None),
    ) + (P(),) * 12
    out_specs = P("ens", "sy", sx, None, None)
    return jax.shard_map(local, mesh=inner, in_specs=in_specs, out_specs=out_specs, check_vma=False)
```

```python
import functools

import jax
import jax.numpy as jnp
from jax import lax
from jax.experimental import pallas as pl
from jax.experimental.pallas import tpu as pltpu
from jax.sharding import Mesh, PartitionSpec as P

F32 = jnp.float32
BF16 = jnp.bfloat16
VMEM = pl.BlockSpec(memory_space=pltpu.VMEM)
HBM = pl.BlockSpec(memory_space=pltpu.HBM)
MIB = 1024 * 1024


def dot(a, b):
    return lax.dot_general(a, b, (((1,), (0,)), ((), ())), preferred_element_type=F32)


def dot_t(a, b):
    return lax.dot_general(a, b, (((0,), (0,)), ((), ())), preferred_element_type=F32)


def norm(values, gain):
    center = values - jnp.mean(values, -1, keepdims=True)
    spread = jnp.mean(center * center, -1, keepdims=True)
    return center * lax.rsqrt(spread + 1e-05) * gain


def far(array):
    return pltpu.with_memory_space_constraint(array, pltpu.HBM)


def start_all(pairs, sems):
    copies = [pltpu.make_async_copy(src, dst, sems.at[n]) for n, (src, dst) in enumerate(pairs)]
    for copy in copies:
        copy.start()
    return copies


def cut_kernel(state, last_row, first_row, last_col, first_col, sems):
    pairs = [
        (state.at[:, 1:2], last_row),
        (state.at[:, 0:1], first_row),
        (state.at[:, :, 1:2], last_col),
        (state.at[:, :, 0:1], first_col),
    ]
    for copy in start_all(pairs, sems):
        copy.wait()


def stage_kernel(
    state_in, w_self_in, map_in, nbr_in, adj_in, tiles_in, w_msg_in, w_agg_in, w_out_in, gain_in,
    state, own_part, up_map, nbr, adj, tiles, w_msg, w_agg, w_out, gain, w_self, sems,
):
    pairs = [
        (state_in, state), (w_self_in, w_self), (map_in, up_map), (nbr_in, nbr), (adj_in, adj),
        (tiles_in, tiles), (w_msg_in, w_msg), (w_agg_in, w_agg), (w_out_in, w_out),
        (gain_in, gain),
    ]
    copies = start_all(pairs, sems)
    copies[0].wait()
    copies[1].wait()
    own = jnp.concatenate([state[0, b // 2, b % 2] for b in range(4)], axis=0)
    own_part[...] = dot(own, w_self[...])
    for copy in copies[2:]:
        copy.wait()


def near_kernel(
    map_in, nbr_in, up, down, left, right, state, adj, tiles, top_adj,
    mixed, corner_edges, label, sent, turned, near, away, frame, up_map, nbr, edges, sems,
    *, core_axis,
):
    copies = start_all([(map_in, up_map), (nbr_in, nbr)], sems)
    for c in range(2):
        frame[1 + c] = up[0, 0, c]
        frame[13 + c] = down[0, 0, c]
        for r in range(2):
            frame[(1 + r) * 4 + 1 + c] = state[0, r, c]
    for r in range(2):
        frame[(1 + r) * 4] = left[0, r, 0]
        frame[(1 + r) * 4 + 3] = right[0, r, 0]
        frame[12 * r] = jnp.zeros((128, 256), BF16)
        frame[12 * r + 3] = jnp.zeros((128, 256), BF16)
    for copy in copies:
        copy.wait()
    pairs = [(top_adj.at[up_map[b // 2, b % 2]], edges.at[b]) for b in range(4)]
    copies = start_all(pairs, sems.at[pl.ds(2, 4)])
    lane = lax.broadcasted_iota(jnp.int32, (64, 128), 1)
    block = lane >> 5
    joined = jnp.where(
        block < 2,
        jnp.where(block == 0, up_map[0, 0], up_map[0, 1]),
        jnp.where(block == 2, up_map[1, 0], up_map[1, 1]),
    )
    label[...] = jnp.where((lane & 31) == joined, 1.0, 0.0)
    row = lax.broadcasted_iota(jnp.int32, (128, 128), 0)
    col = lax.broadcasted_iota(jnp.int32, (128, 128), 1)
    want = (row & 1) * 64 + (row & 62) + (row >> 6)
    order = jnp.where(col == want, 1.0, 0.0).astype(BF16)
    for y in range(2):
        for x in range(2):
            b = 2 * y + x
            picked = []
            for k in range(4):
                code = nbr[y, x, k]
                spot = (y + lax.div(code, 3)) * 4 + x + lax.rem(code, 3)
                picked.append(frame[spot])
                tile = adj[y, x, k]
                corner = jnp.where(code == 6 * y + 2 * x, tile, jnp.zeros_like(tile))
                corner_edges[b, :, 128 * k : 128 * k + 128] = corner
            tile_row = jnp.concatenate([adj[y, x, k] for k in range(4)], axis=1)
            mixed[128 * b : 128 * b + 128] = dot(tile_row, jnp.concatenate(picked, axis=0))
    core = lax.axis_index(core_axis)
    for b in range(4):
        turned[b // 2, b % 2] = tiles[b // 2, b % 2].T
        sent[b] = dot(order, tiles[b // 2, b % 2]).astype(BF16)
        copies[b].wait()
        low = jnp.concatenate([edges[b, k][:, :64] for k in range(4)], axis=1)
        high = jnp.concatenate([edges[b, k][:, 64:] for k in range(4)], axis=1)
        near[b] = jnp.where(core == 0, low, high)
        away[b] = jnp.where(core == 0, high, low)


def fine_kernel(
    corner_l, corner_r, mixed_in, corner_edges, label, sent, state, own_part,
    w_msg, w_agg, w_out, gain, fine_out, piece_out, lines,
):
    own, mixed = [], []
    for y in range(2):
        for x in range(2):
            b = 2 * y + x
            corner = (corner_r if x else corner_l)[1 - y]
            picked = jnp.concatenate([corner] * 4, axis=0)
            total = mixed_in[128 * b : 128 * b + 128] + dot(corner_edges[b], picked)
            mixed.append(total.astype(BF16))
            own.append(state[0, y, x])
    own = jnp.concatenate(own, axis=0)
    mixed = jnp.concatenate(mixed, axis=0)
    agg = dot(mixed, w_msg[...]).astype(BF16)
    hidden = jax.nn.silu(own_part[...] + dot(agg, w_agg[...])).astype(BF16)
    fine = norm(own.astype(F32) + dot(hidden, w_out[...]), gain[...]).astype(BF16)
    fine_out[...] = fine
    for b in range(4):
        contrib = dot(sent[b], fine[b * 128 : (b + 1) * 128])
        for h in range(2):
            for i in range(2):
                part = contrib[64 * i : 64 * i + 64, 128 * h : 128 * h + 128]
                lines[pl.ds(8 * h + 2 * b + i, 64, stride=18), :] = part
    lines[pl.ds(16, 64, stride=18), :] = label[...]
    lines[pl.ds(17, 64, stride=18), :] = jnp.zeros((64, 128), F32)
    piece_out[...] = lines[...].astype(BF16)


def sum_kernel(got, gain, share_out, lines):
    lines[...] = got[...].astype(F32)
    take = lambda n: lines[pl.ds(n, 64, stride=18), :]
    label = take(16)
    member, values = [], []
    for b in range(4):
        member.append(pltpu.roll(label, (128 - 32 * b) % 128, 1) if b else label)
        wide = [take(8 * h + 2 * b + i) for i in range(2) for h in range(2)]
        values.append(jnp.concatenate(wide, axis=1))
    member = jnp.concatenate(member, axis=0).astype(BF16)
    values = jnp.concatenate(values, axis=0).astype(BF16)
    total = dot_t(member, values)[:32]
    both = [norm(total[:, 256 * i : 256 * i + 256], gain[...]) for i in range(2)]
    both = jnp.concatenate(both, axis=0).astype(BF16)
    row = lax.broadcasted_iota(jnp.int32, (40, 64), 0)
    col = lax.broadcasted_iota(jnp.int32, (40, 64), 1)
    order = jnp.where(col == (row & 1) * 32 + (row >> 1), 1.0, 0.0).astype(BF16)
    share = dot(order, both).astype(BF16)
    share_out[...] = jnp.broadcast_to(share[None], share_out.shape)


def order_kernel(got, out):
    row = lax.broadcasted_iota(jnp.int32, (160, 160), 0)
    col = lax.broadcasted_iota(jnp.int32, (160, 160), 1)
    want = ((row & 7) >> 1) * 40 + (row >> 3) * 2 + (row & 1)
    order = jnp.where(col == want, 1.0, 0.0).astype(BF16)
    moved = [dot(order, got[4 * h : 4 * h + 4].reshape(160, 256)) for h in range(2)]
    moved = jnp.concatenate([part.reshape(20, 8, 256) for part in moved], axis=1)
    out[...] = jnp.broadcast_to(moved.astype(BF16)[None], out.shape)


def half_block(source, at):
    return jnp.concatenate([source[x, at] for x in range(4)], axis=0)


def gather_parts(up_map, top_nbr, edges, source):
    mixed = []
    for b in range(4):
        at = up_map[b // 2, b % 2]
        picked = jnp.concatenate([half_block(source, top_nbr[k, at]) for k in range(4)], axis=0)
        mixed.append(dot(edges[b], picked))
    return jnp.concatenate(mixed, axis=0)


def half_kernel(map_in, nbr_in, mine, near, mixed, chosen, up_map, top_nbr, sems):
    for copy in start_all([(map_in, up_map), (nbr_in, top_nbr)], sems):
        copy.wait()
    for b in range(4):
        chosen[b] = half_block(mine, up_map[b // 2, b % 2])
    mixed[...] = gather_parts(up_map, top_nbr, near, mine)


def top_kernel(
    map_in, nbr_in, other, away, mixed, chosen, fine, turned, w_msg, w_agg, w_down, gain,
    out, whole, up_map, top_nbr, sems, *, core_axis,
):
    copies = start_all([(map_in, up_map), (nbr_in, top_nbr)], sems)
    core = lax.axis_index(core_axis)
    here = pl.ds(pl.multiple_of(core * 64, 64), 64)
    there = pl.ds(pl.multiple_of((1 - core) * 64, 64), 64)
    for b in range(4):
        whole[b, here, :] = chosen[b]
    for copy in copies:
        copy.wait()
    for b in range(4):
        whole[b, there, :] = half_block(other, up_map[b // 2, b % 2])
    both = mixed[...] + gather_parts(up_map, top_nbr, away, other)
    tagg = dot(both.astype(BF16), w_msg[...]).astype(BF16)
    zero = jnp.concatenate([whole[b] for b in range(4)], axis=0).astype(F32)
    one = (zero + jax.nn.silu(dot(tagg, w_agg[...]))).astype(BF16)
    copies = []
    for b in range(4):
        rows = slice(b * 128, (b + 1) * 128)
        lower = dot(turned[b // 2, b % 2], one[rows]).astype(BF16)
        final = norm(fine[rows].astype(F32) + dot(lower, w_down[...]), gain[...])
        whole[b] = final.astype(BF16)
        copy = pltpu.make_async_copy(whole.at[b], out.at[0, b // 2, b % 2], sems.at[2 + b])
        copy.start()
        copies.append(copy)
    for copy in copies:
        copy.wait()


def call(body, ins, outs, scratch, name, busy=0, limit=24, place=VMEM):
    return pl.pallas_call(
        body,
        out_shape=tuple(jax.ShapeDtypeStruct(shape, kind) for shape, kind in outs),
        in_specs=ins,
        out_specs=(place,) * len(outs),
        scratch_shapes=scratch,
        compiler_params=pltpu.CompilerParams(vmem_limit_bytes=limit * MIB),
        cost_estimate=pl.CostEstimate(flops=0, bytes_accessed=busy, transcendentals=0),
        name=name,
    )


def local(
    fine_state, fine_adj, fine_nbr, up_map, up_tiles, top_adj, top_nbr, w_fine_msg, w_fine_self,
    w_fine_agg, w_fine_out, w_top_msg, w_top_agg, w_down, fine_gain, top_gain, out_gain,
):
    sx = ("x", "core")
    rows, cols = lax.axis_size("sy"), lax.axis_size("x") * lax.axis_size("core")
    east = [(i, (i + 1) % cols) for i in range(cols)]
    west = [(j, i) for i, j in east]
    twin = [(0, 1), (1, 0)]
    south = [(i, i + 1) for i in range(rows - 1)]
    north = [(j, i) for i, j in south]
    weight = ((256, 256), BF16)
    tile_set = ((2, 2, 128, 128), BF16)
    part = ((512, 256), F32)
    gain = ((1, 256), F32)
    row_cut, col_cut = ((1, 1, 2, 128, 256), BF16), ((1, 2, 1, 128, 256), BF16)
    dma = pltpu.SemaphoreType.DMA
    last_row, first_row, last_col, first_col = call(
        cut_kernel, [HBM], [row_cut, row_cut, col_cut, col_cut], [dma((4,))], "cut", 1 << 20
    )(far(fine_state))
    down = lax.ppermute(first_row, "sy", north)
    up = lax.ppermute(last_row, "sy", south)
    left = lax.ppermute(last_col, sx, east)
    right = lax.ppermute(first_col, sx, west)
    half_set = ((4, 128, 256), BF16)
    staged = [
        up_map, fine_nbr, fine_adj, up_tiles, w_fine_msg, w_fine_agg, w_fine_out, fine_gain[None],
    ]
    held = call(
        stage_kernel,
        [HBM] * 10,
        [(fine_state.shape, BF16), part] + [(array.shape, array.dtype) for array in staged],
        [pltpu.VMEM(*weight), dma((10,))],
        "stage",
        1 << 23,
    )(*[far(array) for array in [fine_state, w_fine_self] + staged])
    down, up, held = lax.optimization_barrier((down, up, held))
    corner_l = lax.ppermute(jnp.concatenate([down[0, :, 1], up[0, :, 1]]), sx, east)
    corner_r = lax.ppermute(jnp.concatenate([down[0, :, 0], up[0, :, 0]]), sx, west)
    state, own_part, map_here, nbr_here, adj, tiles, *weights = held
    mixed, corner_edges, label, sent, turned, near, away = call(
        functools.partial(near_kernel, core_axis="core"),
        [VMEM] * 9 + [HBM],
        [
            part, ((4, 128, 512), BF16), ((64, 128), F32), ((4, 128, 128), BF16), tile_set,
            half_set, half_set,
        ],
        [
            pltpu.VMEM((16, 128, 256), BF16), pltpu.SMEM((2, 2), jnp.int32),
            pltpu.SMEM((2, 2, 4), jnp.int32), pltpu.VMEM((4, 4, 128, 128), BF16), dma((6,)),
        ],
        "near",
        1 << 23,
    )(map_here, nbr_here, up, down, left, right, state, adj, tiles, far(top_adj))
    fine, piece = call(
        fine_kernel,
        [VMEM] * 12,
        [((512, 256), BF16), ((64 * 18, 128), BF16)],
        [pltpu.VMEM((64 * 18, 128), F32)],
        "fine_level",
        1 << 23,
    )(corner_l, corner_r, mixed, corner_edges, label, sent, state, own_part, *weights)
    piece = piece.reshape(64, 9, 2, 128)
    chips = lax.axis_size("x") * rows
    back = [2 * chip + core for chip in range(chips - 1, -1, -1) for core in range(2)]
    got = lax.all_to_all(piece, ("x", "sy", "core"), 0, 0, axis_index_groups=[back])
    (share,) = call(
        sum_kernel,
        [VMEM] * 2,
        [((8, 40, 256), BF16)],
        [pltpu.VMEM((64 * 18, 128), F32)],
        "top_sum",
        1 << 20,
    )(got.reshape(64 * 18, 128), top_gain[None])
    column = lax.all_to_all(share, "sy", 0, 0, axis_index_groups=[list(range(rows - 1, -1, -1))])
    (column,) = call(
        order_kernel, [VMEM], [((4, 20, 16, 256), BF16)], [], "top_order", 1 << 20
    )(column)
    mine = lax.all_to_all(column, "x", 0, 0, axis_index_groups=[list(range(cols // 2 - 1, -1, -1))])
    other = lax.ppermute(mine, "core", twin)
    tables = [pltpu.SMEM((2, 2), jnp.int32), pltpu.SMEM((4, 20), jnp.int32)]
    mixed, chosen = call(
        half_kernel,
        [HBM] * 2 + [VMEM] * 2,
        [part, ((4, 64, 256), BF16)],
        tables + [dma((2,))],
        "top_half",
        1 << 23,
    )(up_map, top_nbr.T, mine, near)
    (out,) = call(
        functools.partial(top_kernel, core_axis="core"),
        [HBM] * 2 + [VMEM] * 10,
        [(fine_state.shape, BF16)],
        [pltpu.VMEM(*half_set)] + tables + [dma((6,))],
        "top_level",
        1 << 23,
        place=HBM,
    )(
        up_map, top_nbr.T, other, away, mixed, chosen, fine, turned, w_top_msg, w_top_agg,
        w_down, out_gain[None],
    )
    return out


def solution(mesh):
    shape = dict(mesh.shape)
    inner = Mesh(
        mesh.devices.reshape(shape["ens"], shape["sy"], shape["sx"] // 2, 2),
        ("ens", "sy", "x", "core"),
    )
    sx = ("x", "core")
    in_specs = (
        P("ens", "sy", sx, None, None),
        P("sy", sx, None, None, None),
        P("sy", sx, None),
        P("sy", sx),
        P("sy", sx, None, None),
    ) + (P(),) * 12
    out_specs = P("ens", "sy", sx, None, None)
    return jax.shard_map(local, mesh=inner, in_specs=in_specs, out_specs=out_specs, check_vma=False)
```

```python
import functools

import jax
import jax.numpy as jnp
from jax import lax
from jax.experimental import pallas as pl
from jax.experimental.pallas import tpu as pltpu
from jax.sharding import Mesh, PartitionSpec as P

F32 = jnp.float32
BF16 = jnp.bfloat16
VMEM = pl.BlockSpec(memory_space=pltpu.VMEM)
HBM = pl.BlockSpec(memory_space=pltpu.HBM)
MIB = 1024 * 1024


def dot(a, b):
    return lax.dot_general(a, b, (((1,), (0,)), ((), ())), preferred_element_type=F32)


def dot_t(a, b):
    return lax.dot_general(a, b, (((0,), (0,)), ((), ())), preferred_element_type=F32)


def norm(values, gain):
    center = values - jnp.mean(values, -1, keepdims=True)
    spread = jnp.mean(center * center, -1, keepdims=True)
    return center * lax.rsqrt(spread + 1e-05) * gain


def far(array):
    return pltpu.with_memory_space_constraint(array, pltpu.HBM)


def start_all(pairs, sems):
    copies = [pltpu.make_async_copy(src, dst, sems.at[n]) for n, (src, dst) in enumerate(pairs)]
    for copy in copies:
        copy.start()
    return copies


def cut_kernel(state, last_row, first_row, last_col, first_col, sems):
    pairs = [
        (state.at[:, 1:2], last_row),
        (state.at[:, 0:1], first_row),
        (state.at[:, :, 1:2], last_col),
        (state.at[:, :, 0:1], first_col),
    ]
    for copy in start_all(pairs, sems):
        copy.wait()


def stage_kernel(
    state_in, w_self_in, map_in, nbr_in, adj_in, tiles_in, w_msg_in, w_agg_in, w_out_in, gain_in,
    state, own_part, up_map, nbr, adj, tiles, w_msg, w_agg, w_out, gain, w_self, sems,
):
    pairs = [
        (state_in, state), (w_self_in, w_self), (map_in, up_map), (nbr_in, nbr), (adj_in, adj),
        (tiles_in, tiles), (w_msg_in, w_msg), (w_agg_in, w_agg), (w_out_in, w_out),
        (gain_in, gain),
    ]
    copies = start_all(pairs, sems)
    copies[0].wait()
    copies[1].wait()
    own = jnp.concatenate([state[0, b // 2, b % 2] for b in range(4)], axis=0)
    own_part[...] = dot(own, w_self[...])
    for copy in copies[2:]:
        copy.wait()


def near_kernel(
    up_map, nbr, up, down, right, left, state, adj, tiles, top_nbr_in, top_adj,
    mixed, corner_edges, label, sent, turned, near, away, picks, frame, top_nbr, edges, sems,
    *, core_axis,
):
    table = pltpu.make_async_copy(top_nbr_in, top_nbr, sems.at[4])
    table.start()
    joins = [up_map[...][b // 2, b % 2] for b in range(4)]
    copies = start_all([(top_adj.at[joins[b]], edges.at[b]) for b in range(4)], sems)
    for c in range(2):
        frame[1 + c] = up[0, 0, c]
        frame[13 + c] = down[0, 0, c]
        for r in range(2):
            frame[(1 + r) * 4 + 1 + c] = state[0, r, c]
    for r in range(2):
        frame[(1 + r) * 4] = left[0, r, 0]
        frame[(1 + r) * 4 + 3] = right[0, r, 0]
        frame[12 * r] = jnp.zeros((128, 256), BF16)
        frame[12 * r + 3] = jnp.zeros((128, 256), BF16)
    lane = lax.broadcasted_iota(jnp.int32, (64, 128), 1)
    block = lane >> 5
    joined = jnp.where(
        block < 2,
        jnp.where(block == 0, joins[0], joins[1]),
        jnp.where(block == 2, joins[2], joins[3]),
    )
    label[...] = jnp.where((lane & 31) == joined, 1.0, 0.0)
    row = lax.broadcasted_iota(jnp.int32, (128, 128), 0)
    col = lax.broadcasted_iota(jnp.int32, (128, 128), 1)
    want = (row & 1) * 64 + (row & 62) + (row >> 6)
    order = jnp.where(col == want, 1.0, 0.0).astype(BF16)
    for y in range(2):
        for x in range(2):
            b = 2 * y + x
            picked = []
            for k in range(4):
                code = nbr[y][x, k]
                spot = (y + lax.div(code, 3)) * 4 + x + lax.rem(code, 3)
                picked.append(frame[spot])
                tile = adj[y, x, k]
                corner = jnp.where(code == 6 * y + 2 * x, tile, jnp.zeros_like(tile))
                corner_edges[b, :, 128 * k : 128 * k + 128] = corner
            tile_row = jnp.concatenate([adj[y, x, k] for k in range(4)], axis=1)
            mixed[128 * b : 128 * b + 128] = dot(tile_row, jnp.concatenate(picked, axis=0))
    core = lax.axis_index(core_axis)
    for b in range(4):
        turned[b // 2, b % 2] = tiles[b // 2, b % 2].T
        sent[b] = dot(order, tiles[b // 2, b % 2]).astype(BF16)
        copies[b].wait()
        low = jnp.concatenate([edges[b, k][:, :64] for k in range(4)], axis=1)
        high = jnp.concatenate([edges[b, k][:, 64:] for k in range(4)], axis=1)
        near[b] = jnp.where(core == 0, low, high)
        away[b] = jnp.where(core == 0, high, low)
    table.wait()
    for b in range(4):
        picks[pl.ds(b, 1), :] = jnp.full((1, 128), joins[b], jnp.int32)
        for k in range(4):
            source = jnp.full((1, 128), top_nbr[k, joins[b]], jnp.int32)
            picks[pl.ds(4 + 4 * b + k, 1), :] = source


def fine_kernel(
    corner_l, corner_r, mixed_in, corner_edges, label, sent, state, own_part,
    w_msg, w_agg, w_out, gain, fine_out, piece_out, lines,
):
    own, mixed = [], []
    for y in range(2):
        for x in range(2):
            b = 2 * y + x
            corner = (corner_r if x else corner_l)[1 - y]
            picked = jnp.concatenate([corner] * 4, axis=0)
            total = mixed_in[128 * b : 128 * b + 128] + dot(corner_edges[b], picked)
            mixed.append(total.astype(BF16))
            own.append(state[0, y, x])
    own = jnp.concatenate(own, axis=0)
    mixed = jnp.concatenate(mixed, axis=0)
    agg = dot(mixed, w_msg[...]).astype(BF16)
    hidden = jax.nn.silu(own_part[...] + dot(agg, w_agg[...])).astype(BF16)
    fine = norm(own.astype(F32) + dot(hidden, w_out[...]), gain[...]).astype(BF16)
    fine_out[...] = fine
    for b in range(4):
        contrib = dot(sent[b], fine[b * 128 : (b + 1) * 128])
        for h in range(2):
            for i in range(2):
                part = contrib[64 * i : 64 * i + 64, 128 * h : 128 * h + 128]
                lines[pl.ds(8 * h + 2 * b + i, 64, stride=18), :] = part
    lines[pl.ds(16, 64, stride=18), :] = label[...]
    lines[pl.ds(17, 64, stride=18), :] = jnp.zeros((64, 128), F32)
    piece_out[...] = lines[...].astype(BF16)


def sum_kernel(got, gain, share_out, lines):
    lines[...] = got[...].astype(F32)
    take = lambda n: lines[pl.ds(n, 64, stride=18), :]
    label = take(16)
    member, values = [], []
    for b in range(4):
        member.append(pltpu.roll(label, (128 - 32 * b) % 128, 1) if b else label)
        wide = [take(8 * h + 2 * b + i) for i in range(2) for h in range(2)]
        values.append(jnp.concatenate(wide, axis=1))
    member = jnp.concatenate(member, axis=0).astype(BF16)
    values = jnp.concatenate(values, axis=0).astype(BF16)
    total = dot_t(member, values)[:32]
    both = [norm(total[:, 256 * i : 256 * i + 256], gain[...]) for i in range(2)]
    both = jnp.concatenate(both, axis=0).astype(BF16)
    row = lax.broadcasted_iota(jnp.int32, (40, 64), 0)
    col = lax.broadcasted_iota(jnp.int32, (40, 64), 1)
    order = jnp.where(col == (row & 1) * 32 + (row >> 1), 1.0, 0.0).astype(BF16)
    share = dot(order, both).astype(BF16)
    share_out[...] = jnp.broadcast_to(share[None], share_out.shape)


def order_kernel(got, out):
    row = lax.broadcasted_iota(jnp.int32, (160, 160), 0)
    col = lax.broadcasted_iota(jnp.int32, (160, 160), 1)
    want = ((row & 7) >> 1) * 40 + (row >> 3) * 2 + (row & 1)
    order = jnp.where(col == want, 1.0, 0.0).astype(BF16)
    moved = [dot(order, got[4 * h : 4 * h + 4].reshape(160, 256)) for h in range(2)]
    moved = jnp.concatenate([part.reshape(20, 8, 256) for part in moved], axis=1)
    out[...] = jnp.broadcast_to(moved.astype(BF16)[None], out.shape)


def half_block(source, at):
    return jnp.concatenate([source[x, at] for x in range(4)], axis=0)


def pick(picks, line):
    return picks[pl.ds(line, 1), pl.ds(0, 1)][0, 0]


def gather_parts(picks, edges, source):
    mixed = []
    for b in range(4):
        picked = [half_block(source, pick(picks, 4 + 4 * b + k)) for k in range(4)]
        mixed.append(dot(edges[b], jnp.concatenate(picked, axis=0)))
    return jnp.concatenate(mixed, axis=0)


def half_kernel(picks, mine, near, mixed, chosen):
    for b in range(4):
        chosen[b] = half_block(mine, pick(picks, b))
    mixed[...] = gather_parts(picks, near, mine)


def top_kernel(
    picks, other, away, mixed, chosen, fine, turned, w_msg, w_agg, w_down, gain,
    out, whole, sems, *, core_axis,
):
    core = lax.axis_index(core_axis)
    here = pl.ds(pl.multiple_of(core * 64, 64), 64)
    there = pl.ds(pl.multiple_of((1 - core) * 64, 64), 64)
    for b in range(4):
        whole[b, here, :] = chosen[b]
        whole[b, there, :] = half_block(other, pick(picks, b))
    both = mixed[...] + gather_parts(picks, away, other)
    tagg = dot(both.astype(BF16), w_msg[...]).astype(BF16)
    zero = jnp.concatenate([whole[b] for b in range(4)], axis=0).astype(F32)
    one = (zero + jax.nn.silu(dot(tagg, w_agg[...]))).astype(BF16)
    copies = []
    for b in range(4):
        rows = slice(b * 128, (b + 1) * 128)
        lower = dot(turned[b // 2, b % 2], one[rows]).astype(BF16)
        final = norm(fine[rows].astype(F32) + dot(lower, w_down[...]), gain[...])
        whole[b] = final.astype(BF16)
        copy = pltpu.make_async_copy(whole.at[b], out.at[0, b // 2, b % 2], sems.at[b])
        copy.start()
        copies.append(copy)
    for copy in copies:
        copy.wait()


def call(body, ins, outs, scratch, name, busy=0, limit=24, place=VMEM):
    return pl.pallas_call(
        body,
        out_shape=tuple(jax.ShapeDtypeStruct(shape, kind) for shape, kind in outs),
        in_specs=ins,
        out_specs=(place,) * len(outs),
        scratch_shapes=scratch,
        compiler_params=pltpu.CompilerParams(vmem_limit_bytes=limit * MIB),
        cost_estimate=pl.CostEstimate(flops=0, bytes_accessed=busy, transcendentals=0),
        name=name,
    )


def local(
    fine_state, fine_adj, fine_nbr, up_map, up_tiles, top_adj, top_nbr, w_fine_msg, w_fine_self,
    w_fine_agg, w_fine_out, w_top_msg, w_top_agg, w_down, fine_gain, top_gain, out_gain,
):
    sx = ("x", "core")
    rows, cols = lax.axis_size("sy"), lax.axis_size("x") * lax.axis_size("core")
    east = [(i, (i + 1) % cols) for i in range(cols)]
    west = [(j, i) for i, j in east]
    twin = [(0, 1), (1, 0)]
    south = [(i, i + 1) for i in range(rows - 1)]
    north = [(j, i) for i, j in south]
    weight = ((256, 256), BF16)
    tile_set = ((2, 2, 128, 128), BF16)
    part = ((512, 256), F32)
    gain = ((1, 256), F32)
    row_cut, col_cut = ((1, 1, 2, 128, 256), BF16), ((1, 2, 1, 128, 256), BF16)
    dma = pltpu.SemaphoreType.DMA
    last_row, first_row, last_col, first_col = call(
        cut_kernel, [HBM], [row_cut, row_cut, col_cut, col_cut], [dma((4,))], "cut", 1 << 20
    )(far(fine_state))
    down = lax.ppermute(first_row, "sy", north)
    up = lax.ppermute(last_row, "sy", south)
    left = lax.ppermute(last_col, sx, east)
    right = lax.ppermute(first_col, sx, west)
    half_set = ((4, 128, 256), BF16)
    staged = [
        up_map, fine_nbr, fine_adj, up_tiles, w_fine_msg, w_fine_agg, w_fine_out, fine_gain[None],
    ]
    held = call(
        stage_kernel,
        [HBM] * 10,
        [(fine_state.shape, BF16), part] + [(array.shape, array.dtype) for array in staged],
        [pltpu.VMEM(*weight), dma((10,))],
        "stage",
        1 << 23,
    )(*[far(array) for array in [fine_state, w_fine_self] + staged])
    down, up, held = lax.optimization_barrier((down, up, held))
    corner_l = lax.ppermute(jnp.concatenate([down[0, :, 1], up[0, :, 1]]), sx, east)
    corner_r = lax.ppermute(jnp.concatenate([down[0, :, 0], up[0, :, 0]]), sx, west)
    state, own_part, map_here, nbr_here, adj, tiles, *weights = held
    mixed, corner_edges, label, sent, turned, near, away, picks = call(
        functools.partial(near_kernel, core_axis="core"),
        [VMEM] * 9 + [HBM] * 2,
        [
            part, ((4, 128, 512), BF16), ((64, 128), F32), ((4, 128, 128), BF16), tile_set,
            half_set, half_set, ((32, 128), jnp.int32),
        ],
        [
            pltpu.VMEM((16, 128, 256), BF16), pltpu.SMEM((4, 20), jnp.int32),
            pltpu.VMEM((4, 4, 128, 128), BF16), dma((5,)),
        ],
        "near",
        1 << 23,
    )(map_here, nbr_here, up, down, right, left, state, adj, tiles, far(top_nbr.T), far(top_adj))
    fine, piece = call(
        fine_kernel,
        [VMEM] * 12,
        [((512, 256), BF16), ((64 * 18, 128), BF16)],
        [pltpu.VMEM((64 * 18, 128), F32)],
        "fine_level",
        1 << 23,
    )(corner_l, corner_r, mixed, corner_edges, label, sent, state, own_part, *weights)
    piece = piece.reshape(64, 9, 2, 128)
    chips = lax.axis_size("x") * rows
    back = [2 * chip + core for chip in range(chips - 1, -1, -1) for core in range(2)]
    got = lax.all_to_all(piece, ("x", "sy", "core"), 0, 0, axis_index_groups=[back])
    (share,) = call(
        sum_kernel,
        [VMEM] * 2,
        [((8, 40, 256), BF16)],
        [pltpu.VMEM((64 * 18, 128), F32)],
        "top_sum",
        1 << 20,
    )(got.reshape(64 * 18, 128), top_gain[None])
    column = lax.all_to_all(share, "sy", 0, 0, axis_index_groups=[list(range(rows - 1, -1, -1))])
    (column,) = call(
        order_kernel, [VMEM], [((4, 20, 16, 256), BF16)], [], "top_order", 1 << 20
    )(column)
    mine = lax.all_to_all(column, "x", 0, 0, axis_index_groups=[list(range(cols // 2 - 1, -1, -1))])
    other = lax.ppermute(mine, "core", twin)
    mixed, chosen = call(
        half_kernel, [VMEM] * 3, [part, ((4, 64, 256), BF16)], [], "top_half", 1 << 23
    )(picks, mine, near)
    (out,) = call(
        functools.partial(top_kernel, core_axis="core"),
        [VMEM] * 11,
        [(fine_state.shape, BF16)],
        [pltpu.VMEM(*half_set), dma((4,))],
        "top_level",
        1 << 23,
        place=HBM,
    )(
        picks, other, away, mixed, chosen, fine, turned, w_top_msg, w_top_agg, w_down,
        out_gain[None],
    )
    return out


def solution(mesh):
    shape = dict(mesh.shape)
    inner = Mesh(
        mesh.devices.reshape(shape["ens"], shape["sy"], shape["sx"] // 2, 2),
        ("ens", "sy", "x", "core"),
    )
    sx = ("x", "core")
    in_specs = (
        P("ens", "sy", sx, None, None),
        P("sy", sx, None, None, None),
        P("sy", sx, None),
        P("sy", sx),
        P("sy", sx, None, None),
    ) + (P(),) * 12
    out_specs = P("ens", "sy", sx, None, None)
    return jax.shard_map(local, mesh=inner, in_specs=in_specs, out_specs=out_specs, check_vma=False)
```

```python
import functools

import jax
import jax.numpy as jnp
from jax import lax
from jax.experimental import pallas as pl
from jax.experimental.pallas import tpu as pltpu
from jax.sharding import Mesh, PartitionSpec as P

F32 = jnp.float32
BF16 = jnp.bfloat16
VMEM = pl.BlockSpec(memory_space=pltpu.VMEM)
HBM = pl.BlockSpec(memory_space=pltpu.HBM)
MIB = 1024 * 1024


def dot(a, b):
    return lax.dot_general(a, b, (((1,), (0,)), ((), ())), preferred_element_type=F32)


def dot_t(a, b):
    return lax.dot_general(a, b, (((0,), (0,)), ((), ())), preferred_element_type=F32)


def norm(values, gain):
    center = values - jnp.mean(values, -1, keepdims=True)
    spread = jnp.mean(center * center, -1, keepdims=True)
    return center * lax.rsqrt(spread + 1e-05) * gain


def far(array):
    return pltpu.with_memory_space_constraint(array, pltpu.HBM)


def start_all(pairs, sems):
    copies = [pltpu.make_async_copy(src, dst, sems.at[n]) for n, (src, dst) in enumerate(pairs)]
    for copy in copies:
        copy.start()
    return copies


def cut_kernel(state, map_in, last_row, first_row, last_col, first_col, up_map, sems):
    pairs = [(map_in, up_map), (state.at[:, 1:2], last_row), (state.at[:, 0:1], first_row)]
    for r in range(2):
        pairs.append((state.at[0, r, 1], last_col.at[pl.ds(128 * r, 128)]))
        pairs.append((state.at[0, r, 0], first_col.at[pl.ds(128 * r, 128)]))
    copies = start_all(pairs, sems)
    copies[0].wait()
    joins = up_map[...]
    line = lax.broadcasted_iota(jnp.int32, (16, 256), 0)
    value = jnp.zeros((16, 256), jnp.int32)
    for b in range(4):
        value = jnp.where(line == b, joins[b // 2, b % 2], value)
    value = value.astype(F32).astype(BF16)
    last_col[256:272, :] = value
    first_col[256:272, :] = value
    for copy in copies[1:]:
        copy.wait()


def stage_kernel(
    state_in, w_self_in, map_in, nbr_in, adj_in, tiles_in, w_msg_in, w_agg_in, w_out_in, gain_in,
    state, own_part, up_map, nbr, adj, tiles, w_msg, w_agg, w_out, gain, w_self, sems,
):
    pairs = [
        (state_in, state), (w_self_in, w_self), (map_in, up_map), (nbr_in, nbr), (adj_in, adj),
        (tiles_in, tiles), (w_msg_in, w_msg), (w_agg_in, w_agg), (w_out_in, w_out),
        (gain_in, gain),
    ]
    copies = start_all(pairs, sems)
    copies[0].wait()
    copies[1].wait()
    own = jnp.concatenate([state[0, b // 2, b % 2] for b in range(4)], axis=0)
    own_part[...] = dot(own, w_self[...])
    for copy in copies[2:]:
        copy.wait()


def near_kernel(
    up_map, nbr, up, down, right, left, state, adj, tiles, top_nbr_in, top_adj,
    mixed, corner_edges, label, sent, turned, keep, give, picks, frame, top_nbr, edges, sems,
    *, core_axis,
):
    table = pltpu.make_async_copy(top_nbr_in, top_nbr, sems.at[8])
    table.start()
    core = lax.axis_index(core_axis)
    joins = [up_map[...][b // 2, b % 2] for b in range(4)]
    twin = jnp.where(core == 0, right[256:272, :].astype(F32), left[256:272, :].astype(F32))
    twin = twin.astype(jnp.int32)
    joins += [twin[b, 0] for b in range(4)]
    copies = start_all([(top_adj.at[joins[b]], edges.at[b]) for b in range(8)], sems)
    for c in range(2):
        frame[1 + c] = up[0, 0, c]
        frame[13 + c] = down[0, 0, c]
        for r in range(2):
            frame[(1 + r) * 4 + 1 + c] = state[0, r, c]
    for r in range(2):
        frame[(1 + r) * 4] = left[128 * r : 128 * r + 128, :]
        frame[(1 + r) * 4 + 3] = right[128 * r : 128 * r + 128, :]
        frame[12 * r] = jnp.zeros((128, 256), BF16)
        frame[12 * r + 3] = jnp.zeros((128, 256), BF16)
    lane = lax.broadcasted_iota(jnp.int32, (64, 128), 1)
    block = lane >> 5
    joined = jnp.where(
        block < 2,
        jnp.where(block == 0, joins[0], joins[1]),
        jnp.where(block == 2, joins[2], joins[3]),
    )
    label[...] = jnp.where((lane & 31) == joined, 1.0, 0.0)
    row = lax.broadcasted_iota(jnp.int32, (128, 128), 0)
    col = lax.broadcasted_iota(jnp.int32, (128, 128), 1)
    want = (row & 1) * 64 + (row & 62) + (row >> 6)
    order = jnp.where(col == want, 1.0, 0.0).astype(BF16)
    for y in range(2):
        for x in range(2):
            b = 2 * y + x
            picked = []
            for k in range(4):
                code = nbr[y][x, k]
                spot = (y + lax.div(code, 3)) * 4 + x + lax.rem(code, 3)
                picked.append(frame[spot])
                tile = adj[y, x, k]
                corner = jnp.where(code == 6 * y + 2 * x, tile, jnp.zeros_like(tile))
                corner_edges[b, :, 128 * k : 128 * k + 128] = corner
            tile_row = jnp.concatenate([adj[y, x, k] for k in range(4)], axis=1)
            mixed[128 * b : 128 * b + 128] = dot(tile_row, jnp.concatenate(picked, axis=0))
    for b in range(4):
        turned[b // 2, b % 2] = tiles[b // 2, b % 2].T
        sent[b] = dot(order, tiles[b // 2, b % 2]).astype(BF16)
    for b in range(8):
        copies[b].wait()
        low = jnp.concatenate([edges[b, k][:, :64] for k in range(4)], axis=1)
        high = jnp.concatenate([edges[b, k][:, 64:] for k in range(4)], axis=1)
        (keep if b < 4 else give)[b % 4] = jnp.where(core == 1, low, high)
    table.wait()
    for b in range(8):
        picks[pl.ds(b, 1), :] = jnp.full((1, 128), joins[b], jnp.int32)
        for k in range(4):
            source = jnp.full((1, 128), top_nbr[k, joins[b]], jnp.int32)
            picks[pl.ds(8 + 4 * b + k, 1), :] = source


def fine_kernel(
    corner_l, corner_r, mixed_in, corner_edges, label, sent, state, own_part,
    w_msg, w_agg, w_out, gain, fine_out, piece_out, lines,
):
    own, mixed = [], []
    for y in range(2):
        for x in range(2):
            b = 2 * y + x
            corner = (corner_r if x else corner_l)[1 - y]
            picked = jnp.concatenate([corner] * 4, axis=0)
            total = mixed_in[128 * b : 128 * b + 128] + dot(corner_edges[b], picked)
            mixed.append(total.astype(BF16))
            own.append(state[0, y, x])
    own = jnp.concatenate(own, axis=0)
    mixed = jnp.concatenate(mixed, axis=0)
    agg = dot(mixed, w_msg[...]).astype(BF16)
    hidden = jax.nn.silu(own_part[...] + dot(agg, w_agg[...])).astype(BF16)
    fine = norm(own.astype(F32) + dot(hidden, w_out[...]), gain[...]).astype(BF16)
    fine_out[...] = fine
    for b in range(4):
        contrib = dot(sent[b], fine[b * 128 : (b + 1) * 128])
        for h in range(2):
            for i in range(2):
                part = contrib[64 * i : 64 * i + 64, 128 * h : 128 * h + 128]
                lines[pl.ds(8 * h + 2 * b + i, 64, stride=18), :] = part
    lines[pl.ds(16, 64, stride=18), :] = label[...]
    lines[pl.ds(17, 64, stride=18), :] = jnp.zeros((64, 128), F32)
    piece_out[...] = lines[...].astype(BF16)


def sum_kernel(got, gain, share_out, lines):
    lines[...] = got[...].astype(F32)
    take = lambda n: lines[pl.ds(n, 64, stride=18), :]
    label = take(16)
    member, values = [], []
    for b in range(4):
        member.append(pltpu.roll(label, (128 - 32 * b) % 128, 1) if b else label)
        wide = [take(8 * h + 2 * b + i) for i in range(2) for h in range(2)]
        values.append(jnp.concatenate(wide, axis=1))
    member = jnp.concatenate(member, axis=0).astype(BF16)
    values = jnp.concatenate(values, axis=0).astype(BF16)
    total = dot_t(member, values)[:32]
    both = [norm(total[:, 256 * i : 256 * i + 256], gain[...]) for i in range(2)]
    both = jnp.concatenate(both, axis=0).astype(BF16)
    row = lax.broadcasted_iota(jnp.int32, (40, 64), 0)
    col = lax.broadcasted_iota(jnp.int32, (40, 64), 1)
    order = jnp.where(col == (row & 1) * 32 + (row >> 1), 1.0, 0.0).astype(BF16)
    share = dot(order, both).astype(BF16)
    share_out[...] = jnp.broadcast_to(share[None], share_out.shape)


def order_kernel(got, out):
    row = lax.broadcasted_iota(jnp.int32, (160, 160), 0)
    col = lax.broadcasted_iota(jnp.int32, (160, 160), 1)
    want = ((row & 7) >> 1) * 40 + (row >> 3) * 2 + (row & 1)
    order = jnp.where(col == want, 1.0, 0.0).astype(BF16)
    moved = [dot(order, got[4 * h : 4 * h + 4].reshape(160, 256)) for h in range(2)]
    moved = jnp.concatenate([part.reshape(20, 8, 256) for part in moved], axis=1)
    out[...] = jnp.broadcast_to(moved.astype(BF16)[None], out.shape)


def half_block(source, at):
    return jnp.concatenate([source[x, at] for x in range(4)], axis=0)


def pick(picks, line):
    return picks[pl.ds(line, 1), pl.ds(0, 1)][0, 0]


def gather_parts(picks, first, edges, source):
    mixed = []
    for b in range(4):
        lines = [8 + 4 * (first + b) + k for k in range(4)]
        picked = [half_block(source, pick(picks, line)) for line in lines]
        mixed.append(dot(edges[b], jnp.concatenate(picked, axis=0)))
    return jnp.concatenate(mixed, axis=0)


def give_kernel(picks, mine, give, parcel):
    for b in range(4):
        parcel[512 + 64 * b : 576 + 64 * b, :] = half_block(mine, pick(picks, 4 + b))
    parcel[0:512, :] = gather_parts(picks, 4, give, mine).astype(BF16)


def keep_kernel(picks, mine, keep, mixed, chosen):
    for b in range(4):
        chosen[b] = half_block(mine, pick(picks, b))
    mixed[...] = gather_parts(picks, 0, keep, mine)


def top_kernel(
    parcel, mixed, chosen, fine, turned, w_msg, w_agg, w_down, gain, out, whole, sems, *, core_axis
):
    core = lax.axis_index(core_axis)
    here = pl.ds(pl.multiple_of((1 - core) * 64, 64), 64)
    there = pl.ds(pl.multiple_of(core * 64, 64), 64)
    for b in range(4):
        whole[b, here, :] = chosen[b]
        whole[b, there, :] = parcel[512 + 64 * b : 576 + 64 * b, :]
    both = mixed[...] + parcel[0:512, :].astype(F32)
    tagg = dot(both.astype(BF16), w_msg[...]).astype(BF16)
    zero = jnp.concatenate([whole[b] for b in range(4)], axis=0).astype(F32)
    one = (zero + jax.nn.silu(dot(tagg, w_agg[...]))).astype(BF16)
    copies = []
    for b in range(4):
        rows = slice(b * 128, (b + 1) * 128)
        lower = dot(turned[b // 2, b % 2], one[rows]).astype(BF16)
        final = norm(fine[rows].astype(F32) + dot(lower, w_down[...]), gain[...])
        whole[b] = final.astype(BF16)
        copy = pltpu.make_async_copy(whole.at[b], out.at[0, b // 2, b % 2], sems.at[b])
        copy.start()
        copies.append(copy)
    for copy in copies:
        copy.wait()


def call(body, ins, outs, scratch, name, busy=0, limit=24, place=VMEM):
    return pl.pallas_call(
        body,
        out_shape=tuple(jax.ShapeDtypeStruct(shape, kind) for shape, kind in outs),
        in_specs=ins,
        out_specs=(place,) * len(outs),
        scratch_shapes=scratch,
        compiler_params=pltpu.CompilerParams(vmem_limit_bytes=limit * MIB),
        cost_estimate=pl.CostEstimate(flops=0, bytes_accessed=busy, transcendentals=0),
        name=name,
    )


def local(
    fine_state, fine_adj, fine_nbr, up_map, up_tiles, top_adj, top_nbr, w_fine_msg, w_fine_self,
    w_fine_agg, w_fine_out, w_top_msg, w_top_agg, w_down, fine_gain, top_gain, out_gain,
):
    sx = ("x", "core")
    rows, cols = lax.axis_size("sy"), lax.axis_size("x") * lax.axis_size("core")
    east = [(i, (i + 1) % cols) for i in range(cols)]
    west = [(j, i) for i, j in east]
    twin = [(0, 1), (1, 0)]
    south = [(i, i + 1) for i in range(rows - 1)]
    north = [(j, i) for i, j in south]
    weight = ((256, 256), BF16)
    tile_set = ((2, 2, 128, 128), BF16)
    part = ((512, 256), F32)
    gain = ((1, 256), F32)
    row_cut, col_cut = ((1, 1, 2, 128, 256), BF16), ((272, 256), BF16)
    dma = pltpu.SemaphoreType.DMA
    last_row, first_row, last_col, first_col = call(
        cut_kernel,
        [HBM] * 2,
        [row_cut, row_cut, col_cut, col_cut],
        [pltpu.VMEM((2, 2), jnp.int32), dma((7,))],
        "cut",
        1 << 20,
    )(far(fine_state), far(up_map))
    down = lax.ppermute(first_row, "sy", north)
    up = lax.ppermute(last_row, "sy", south)
    left = lax.ppermute(last_col, sx, east)
    right = lax.ppermute(first_col, sx, west)
    half_set = ((4, 128, 256), BF16)
    staged = [
        up_map, fine_nbr, fine_adj, up_tiles, w_fine_msg, w_fine_agg, w_fine_out, fine_gain[None],
    ]
    held = call(
        stage_kernel,
        [HBM] * 10,
        [(fine_state.shape, BF16), part] + [(array.shape, array.dtype) for array in staged],
        [pltpu.VMEM(*weight), dma((10,))],
        "stage",
        1 << 23,
    )(*[far(array) for array in [fine_state, w_fine_self] + staged])
    down, up, held = lax.optimization_barrier((down, up, held))
    corner_l = lax.ppermute(jnp.concatenate([down[0, :, 1], up[0, :, 1]]), sx, east)
    corner_r = lax.ppermute(jnp.concatenate([down[0, :, 0], up[0, :, 0]]), sx, west)
    state, own_part, map_here, nbr_here, adj, tiles, *weights = held
    mixed, corner_edges, label, sent, turned, keep, give, picks = call(
        functools.partial(near_kernel, core_axis="core"),
        [VMEM] * 9 + [HBM] * 2,
        [
            part, ((4, 128, 512), BF16), ((64, 128), F32), ((4, 128, 128), BF16), tile_set,
            half_set, half_set, ((40, 128), jnp.int32),
        ],
        [
            pltpu.VMEM((16, 128, 256), BF16), pltpu.SMEM((4, 20), jnp.int32),
            pltpu.VMEM((8, 4, 128, 128), BF16), dma((9,)),
        ],
        "near",
        1 << 23,
    )(map_here, nbr_here, up, down, right, left, state, adj, tiles, far(top_nbr.T), far(top_adj))
    fine, piece = call(
        fine_kernel,
        [VMEM] * 12,
        [((512, 256), BF16), ((64 * 18, 128), BF16)],
        [pltpu.VMEM((64 * 18, 128), F32)],
        "fine_level",
        1 << 23,
    )(corner_l, corner_r, mixed, corner_edges, label, sent, state, own_part, *weights)
    piece = piece.reshape(64, 9, 2, 128)
    chips = lax.axis_size("x") * rows
    back = [2 * chip + core for chip in range(chips - 1, -1, -1) for core in (1, 0)]
    got = lax.all_to_all(piece, ("x", "sy", "core"), 0, 0, axis_index_groups=[back])
    (share,) = call(
        sum_kernel,
        [VMEM] * 2,
        [((8, 40, 256), BF16)],
        [pltpu.VMEM((64 * 18, 128), F32)],
        "top_sum",
        1 << 20,
    )(got.reshape(64 * 18, 128), top_gain[None])
    column = lax.all_to_all(share, "sy", 0, 0, axis_index_groups=[list(range(rows - 1, -1, -1))])
    (column,) = call(
        order_kernel, [VMEM], [((4, 20, 16, 256), BF16)], [], "top_order", 1 << 20
    )(column)
    mine = lax.all_to_all(column, "x", 0, 0, axis_index_groups=[list(range(cols // 2 - 1, -1, -1))])
    (parcel,) = call(
        give_kernel, [VMEM] * 3, [((768, 256), BF16)], [], "top_give", 1 << 20
    )(picks, mine, give)
    parcel = lax.ppermute(parcel, "core", twin)
    mixed, chosen = call(
        keep_kernel, [VMEM] * 3, [part, ((4, 64, 256), BF16)], [], "top_keep", 1 << 23
    )(picks, mine, keep)
    (out,) = call(
        functools.partial(top_kernel, core_axis="core"),
        [VMEM] * 9,
        [(fine_state.shape, BF16)],
        [pltpu.VMEM(*half_set), dma((4,))],
        "top_level",
        1 << 23,
        place=HBM,
    )(parcel, mixed, chosen, fine, turned, w_top_msg, w_top_agg, w_down, out_gain[None])
    return out


def solution(mesh):
    shape = dict(mesh.shape)
    inner = Mesh(
        mesh.devices.reshape(shape["ens"], shape["sy"], shape["sx"] // 2, 2),
        ("ens", "sy", "x", "core"),
    )
    sx = ("x", "core")
    in_specs = (
        P("ens", "sy", sx, None, None),
        P("sy", sx, None, None, None),
        P("sy", sx, None),
        P("sy", sx),
        P("sy", sx, None, None),
    ) + (P(),) * 12
    out_specs = P("ens", "sy", sx, None, None)
    return jax.shard_map(local, mesh=inner, in_specs=in_specs, out_specs=out_specs, check_vma=False)
```

```python
import functools

import jax
import jax.numpy as jnp
from jax import lax
from jax.experimental import pallas as pl
from jax.experimental.pallas import tpu as pltpu
from jax.sharding import Mesh, PartitionSpec as P

F32 = jnp.float32
BF16 = jnp.bfloat16
VMEM = pl.BlockSpec(memory_space=pltpu.VMEM)
HBM = pl.BlockSpec(memory_space=pltpu.HBM)
MIB = 1024 * 1024


def dot(a, b):
    return lax.dot_general(a, b, (((1,), (0,)), ((), ())), preferred_element_type=F32)


def dot_t(a, b):
    return lax.dot_general(a, b, (((0,), (0,)), ((), ())), preferred_element_type=F32)


def norm(values, gain):
    center = values - jnp.mean(values, -1, keepdims=True)
    spread = jnp.mean(center * center, -1, keepdims=True)
    return center * lax.rsqrt(spread + 1e-05) * gain


def far(array):
    return pltpu.with_memory_space_constraint(array, pltpu.HBM)


def start_all(pairs, sems):
    copies = [pltpu.make_async_copy(src, dst, sems.at[n]) for n, (src, dst) in enumerate(pairs)]
    for copy in copies:
        copy.start()
    return copies


def cut_kernel(state, map_in, last_row, first_row, last_col, first_col, up_map, sems):
    pairs = [(map_in, up_map), (state.at[:, 1:2], last_row), (state.at[:, 0:1], first_row)]
    for r in range(2):
        pairs.append((state.at[0, r, 1], last_col.at[pl.ds(128 * r, 128)]))
        pairs.append((state.at[0, r, 0], first_col.at[pl.ds(128 * r, 128)]))
    copies = start_all(pairs, sems)
    copies[0].wait()
    joins = up_map[...]
    line = lax.broadcasted_iota(jnp.int32, (16, 256), 0)
    value = jnp.zeros((16, 256), jnp.int32)
    for b in range(4):
        value = jnp.where(line == b, joins[b // 2, b % 2], value)
    value = value.astype(F32).astype(BF16)
    last_col[256:272, :] = value
    first_col[256:272, :] = value
    for copy in copies[1:]:
        copy.wait()


def stage_kernel(
    state_in, w_self_in, map_in, nbr_in, adj_in, tiles_in, w_msg_in, w_agg_in, w_out_in, gain_in,
    state, own_part, up_map, nbr, adj, tiles, w_msg, w_agg, w_out, gain, w_self, sems,
):
    pairs = [
        (state_in, state), (w_self_in, w_self), (map_in, up_map), (nbr_in, nbr), (adj_in, adj),
        (tiles_in, tiles), (w_msg_in, w_msg), (w_agg_in, w_agg), (w_out_in, w_out),
        (gain_in, gain),
    ]
    copies = start_all(pairs, sems)
    copies[0].wait()
    copies[1].wait()
    own = jnp.concatenate([state[0, b // 2, b % 2] for b in range(4)], axis=0)
    own_part[...] = dot(own, w_self[...])
    for copy in copies[2:]:
        copy.wait()


def near_kernel(
    up_map, nbr, up, down, right, left, state, adj, tiles, top_nbr_in, top_adj,
    mixed, corner_edges, label, sent, turned, keep, give, picks, frame, top_nbr, edges, sems,
    *, core_axis,
):
    table = pltpu.make_async_copy(top_nbr_in, top_nbr, sems.at[8])
    table.start()
    core = lax.axis_index(core_axis)
    joins = [up_map[...][b // 2, b % 2] for b in range(4)]
    twin = jnp.where(core == 0, right[256:272, :].astype(F32), left[256:272, :].astype(F32))
    twin = twin.astype(jnp.int32)
    joins += [twin[b, 0] for b in range(4)]
    copies = start_all([(top_adj.at[joins[b]], edges.at[b]) for b in range(8)], sems)
    for c in range(2):
        frame[1 + c] = up[0, 0, c]
        frame[13 + c] = down[0, 0, c]
        for r in range(2):
            frame[(1 + r) * 4 + 1 + c] = state[0, r, c]
    for r in range(2):
        frame[(1 + r) * 4] = left[128 * r : 128 * r + 128, :]
        frame[(1 + r) * 4 + 3] = right[128 * r : 128 * r + 128, :]
        frame[12 * r] = jnp.zeros((128, 256), BF16)
        frame[12 * r + 3] = jnp.zeros((128, 256), BF16)
    lane = lax.broadcasted_iota(jnp.int32, (64, 128), 1)
    for j in range(2):
        joined = jnp.where(lane < 64, joins[2 * j], joins[2 * j + 1])
        label[j] = jnp.where((lane & 63) == 2 * joined, 1.0, 0.0)
    row = lax.broadcasted_iota(jnp.int32, (128, 128), 0)
    col = lax.broadcasted_iota(jnp.int32, (128, 128), 1)
    want = (row & 1) * 64 + (row & 62) + (row >> 6)
    order = jnp.where(col == want, 1.0, 0.0).astype(BF16)
    for y in range(2):
        for x in range(2):
            b = 2 * y + x
            picked = []
            for k in range(4):
                code = nbr[y][x, k]
                spot = (y + lax.div(code, 3)) * 4 + x + lax.rem(code, 3)
                picked.append(frame[spot])
                tile = adj[y, x, k]
                corner = jnp.where(code == 6 * y + 2 * x, tile, jnp.zeros_like(tile))
                corner_edges[b, :, 128 * k : 128 * k + 128] = corner
            tile_row = jnp.concatenate([adj[y, x, k] for k in range(4)], axis=1)
            mixed[128 * b : 128 * b + 128] = dot(tile_row, jnp.concatenate(picked, axis=0))
    for b in range(4):
        turned[b // 2, b % 2] = tiles[b // 2, b % 2].T
        sent[b] = dot(order, tiles[b // 2, b % 2]).astype(BF16)
    for b in range(8):
        copies[b].wait()
        low = jnp.concatenate([edges[b, k][:, :64] for k in range(4)], axis=1)
        high = jnp.concatenate([edges[b, k][:, 64:] for k in range(4)], axis=1)
        (keep if b < 4 else give)[b % 4] = jnp.where(core == 1, low, high)
    table.wait()
    for b in range(8):
        picks[pl.ds(b, 1), :] = jnp.full((1, 128), joins[b], jnp.int32)
        for k in range(4):
            source = jnp.full((1, 128), top_nbr[k, joins[b]], jnp.int32)
            picks[pl.ds(8 + 4 * b + k, 1), :] = source


def fine_kernel(
    corner_l, corner_r, mixed_in, corner_edges, label, sent, state, own_part,
    w_msg, w_agg, w_out, gain, fine_out, piece_out, lines,
):
    own, mixed = [], []
    for y in range(2):
        for x in range(2):
            b = 2 * y + x
            corner = (corner_r if x else corner_l)[1 - y]
            picked = jnp.concatenate([corner] * 4, axis=0)
            total = mixed_in[128 * b : 128 * b + 128] + dot(corner_edges[b], picked)
            mixed.append(total.astype(BF16))
            own.append(state[0, y, x])
    own = jnp.concatenate(own, axis=0)
    mixed = jnp.concatenate(mixed, axis=0)
    agg = dot(mixed, w_msg[...]).astype(BF16)
    hidden = jax.nn.silu(own_part[...] + dot(agg, w_agg[...])).astype(BF16)
    fine = norm(own.astype(F32) + dot(hidden, w_out[...]), gain[...]).astype(BF16)
    fine_out[...] = fine
    for b in range(4):
        contrib = dot(sent[b], fine[b * 128 : (b + 1) * 128])
        for h in range(2):
            for i in range(2):
                part = contrib[64 * i : 64 * i + 64, 128 * h : 128 * h + 128]
                lines[pl.ds(8 * h + 2 * b + i, 64, stride=18), :] = part
    for j in range(2):
        lines[pl.ds(16 + j, 64, stride=18), :] = label[j]
    piece_out[...] = lines[0:1152, :].astype(BF16)


def sum_kernel(got, gain, share_out, lines):
    lines[0:1152, :] = got[...].astype(F32)
    take = lambda n: lines[pl.ds(n, 64, stride=18), :]
    labels = [take(16), take(17)]
    member, values = [], []
    for b in range(4):
        for i in range(2):
            turn = 64 * (b % 2) + i
            member.append(pltpu.roll(labels[b // 2], turn, 1) if turn else labels[b // 2])
            wide = [take(8 * h + 2 * b + i) for h in range(2)]
            values.append(jnp.concatenate(wide, axis=1))
    member = jnp.concatenate(member, axis=0).astype(BF16)
    values = jnp.concatenate(values, axis=0).astype(BF16)
    total = dot_t(member, values)[:40]
    share = norm(total, gain[...]).astype(BF16)
    share_out[...] = jnp.broadcast_to(share[None], share_out.shape)


def order_kernel(got, out):
    row = lax.broadcasted_iota(jnp.int32, (160, 160), 0)
    col = lax.broadcasted_iota(jnp.int32, (160, 160), 1)
    want = ((row & 7) >> 1) * 40 + (row >> 3) * 2 + (row & 1)
    order = jnp.where(col == want, 1.0, 0.0).astype(BF16)
    moved = [dot(order, got[4 * h : 4 * h + 4].reshape(160, 256)) for h in range(2)]
    moved = jnp.concatenate([part.reshape(20, 8, 256) for part in moved], axis=1)
    out[...] = jnp.broadcast_to(moved.astype(BF16)[None], out.shape)


def half_block(source, at):
    return jnp.concatenate([source[x, at] for x in range(4)], axis=0)


def pick(picks, line):
    return picks[pl.ds(line, 1), pl.ds(0, 1)][0, 0]


def gather_parts(picks, first, edges, source):
    mixed = []
    for b in range(4):
        lines = [8 + 4 * (first + b) + k for k in range(4)]
        picked = [half_block(source, pick(picks, line)) for line in lines]
        mixed.append(dot(edges[b], jnp.concatenate(picked, axis=0)))
    return jnp.concatenate(mixed, axis=0)


def give_kernel(picks, mine, give, parcel):
    for b in range(4):
        parcel[512 + 64 * b : 576 + 64 * b, :] = half_block(mine, pick(picks, 4 + b))
    parcel[0:512, :] = gather_parts(picks, 4, give, mine).astype(BF16)


def keep_kernel(picks, mine, keep, mixed, chosen):
    for b in range(4):
        chosen[b] = half_block(mine, pick(picks, b))
    mixed[...] = gather_parts(picks, 0, keep, mine)


def top_kernel(
    parcel, mixed, chosen, fine, turned, w_msg, w_agg, w_down, gain, out, whole, sems, *, core_axis
):
    core = lax.axis_index(core_axis)
    here = pl.ds(pl.multiple_of((1 - core) * 64, 64), 64)
    there = pl.ds(pl.multiple_of(core * 64, 64), 64)
    for b in range(4):
        whole[b, here, :] = chosen[b]
        whole[b, there, :] = parcel[512 + 64 * b : 576 + 64 * b, :]
    both = mixed[...] + parcel[0:512, :].astype(F32)
    tagg = dot(both.astype(BF16), w_msg[...]).astype(BF16)
    zero = jnp.concatenate([whole[b] for b in range(4)], axis=0).astype(F32)
    one = (zero + jax.nn.silu(dot(tagg, w_agg[...]))).astype(BF16)
    copies = []
    for b in range(4):
        rows = slice(b * 128, (b + 1) * 128)
        lower = dot(turned[b // 2, b % 2], one[rows]).astype(BF16)
        final = norm(fine[rows].astype(F32) + dot(lower, w_down[...]), gain[...])
        whole[b] = final.astype(BF16)
        copy = pltpu.make_async_copy(whole.at[b], out.at[0, b // 2, b % 2], sems.at[b])
        copy.start()
        copies.append(copy)
    for copy in copies:
        copy.wait()


def call(body, ins, outs, scratch, name, busy=0, limit=24, place=VMEM):
    return pl.pallas_call(
        body,
        out_shape=tuple(jax.ShapeDtypeStruct(shape, kind) for shape, kind in outs),
        in_specs=ins,
        out_specs=(place,) * len(outs),
        scratch_shapes=scratch,
        compiler_params=pltpu.CompilerParams(vmem_limit_bytes=limit * MIB),
        cost_estimate=pl.CostEstimate(flops=0, bytes_accessed=busy, transcendentals=0),
        name=name,
    )


def local(
    fine_state, fine_adj, fine_nbr, up_map, up_tiles, top_adj, top_nbr, w_fine_msg, w_fine_self,
    w_fine_agg, w_fine_out, w_top_msg, w_top_agg, w_down, fine_gain, top_gain, out_gain,
):
    sx = ("x", "core")
    rows, cols = lax.axis_size("sy"), lax.axis_size("x") * lax.axis_size("core")
    east = [(i, (i + 1) % cols) for i in range(cols)]
    west = [(j, i) for i, j in east]
    twin = [(0, 1), (1, 0)]
    south = [(i, i + 1) for i in range(rows - 1)]
    north = [(j, i) for i, j in south]
    weight = ((256, 256), BF16)
    tile_set = ((2, 2, 128, 128), BF16)
    part = ((512, 256), F32)
    gain = ((1, 256), F32)
    row_cut, col_cut = ((1, 1, 2, 128, 256), BF16), ((272, 256), BF16)
    dma = pltpu.SemaphoreType.DMA
    last_row, first_row, last_col, first_col = call(
        cut_kernel,
        [HBM] * 2,
        [row_cut, row_cut, col_cut, col_cut],
        [pltpu.VMEM((2, 2), jnp.int32), dma((7,))],
        "cut",
        1 << 20,
    )(far(fine_state), far(up_map))
    down = lax.ppermute(first_row, "sy", north)
    up = lax.ppermute(last_row, "sy", south)
    left = lax.ppermute(last_col, sx, east)
    right = lax.ppermute(first_col, sx, west)
    half_set = ((4, 128, 256), BF16)
    staged = [
        up_map, fine_nbr, fine_adj, up_tiles, w_fine_msg, w_fine_agg, w_fine_out, fine_gain[None],
    ]
    held = call(
        stage_kernel,
        [HBM] * 10,
        [(fine_state.shape, BF16), part] + [(array.shape, array.dtype) for array in staged],
        [pltpu.VMEM(*weight), dma((10,))],
        "stage",
        1 << 23,
    )(*[far(array) for array in [fine_state, w_fine_self] + staged])
    down, up, held = lax.optimization_barrier((down, up, held))
    corner_l = lax.ppermute(jnp.concatenate([down[0, :, 1], up[0, :, 1]]), sx, east)
    corner_r = lax.ppermute(jnp.concatenate([down[0, :, 0], up[0, :, 0]]), sx, west)
    state, own_part, map_here, nbr_here, adj, tiles, *weights = held
    mixed, corner_edges, label, sent, turned, keep, give, picks = call(
        functools.partial(near_kernel, core_axis="core"),
        [VMEM] * 9 + [HBM] * 2,
        [
            part, ((4, 128, 512), BF16), ((2, 64, 128), F32), ((4, 128, 128), BF16), tile_set,
            half_set, half_set, ((40, 128), jnp.int32),
        ],
        [
            pltpu.VMEM((16, 128, 256), BF16), pltpu.SMEM((4, 20), jnp.int32),
            pltpu.VMEM((8, 4, 128, 128), BF16), dma((9,)),
        ],
        "near",
        1 << 23,
    )(map_here, nbr_here, up, down, right, left, state, adj, tiles, far(top_nbr.T), far(top_adj))
    fine, piece = call(
        fine_kernel,
        [VMEM] * 12,
        [((512, 256), BF16), ((64 * 18, 128), BF16)],
        [pltpu.VMEM((64 * 18 + 24, 128), F32)],
        "fine_level",
        1 << 23,
    )(corner_l, corner_r, mixed, corner_edges, label, sent, state, own_part, *weights)
    piece = piece.reshape(64, 9, 2, 128)
    chips = lax.axis_size("x") * rows
    back = [2 * chip + core for chip in range(chips - 1, -1, -1) for core in (1, 0)]
    got = lax.all_to_all(piece, ("x", "sy", "core"), 0, 0, axis_index_groups=[back])
    (share,) = call(
        sum_kernel,
        [VMEM] * 2,
        [((8, 40, 256), BF16)],
        [pltpu.VMEM((64 * 18 + 24, 128), F32)],
        "top_sum",
        1 << 20,
    )(got.reshape(64 * 18, 128), top_gain[None])
    column = lax.all_to_all(share, "sy", 0, 0, axis_index_groups=[list(range(rows - 1, -1, -1))])
    (column,) = call(
        order_kernel, [VMEM], [((4, 20, 16, 256), BF16)], [], "top_order", 1 << 20
    )(column)
    mine = lax.all_to_all(column, "x", 0, 0, axis_index_groups=[list(range(cols // 2 - 1, -1, -1))])
    (parcel,) = call(
        give_kernel, [VMEM] * 3, [((768, 256), BF16)], [], "top_give", 1 << 20
    )(picks, mine, give)
    parcel = lax.ppermute(parcel, "core", twin)
    mixed, chosen = call(
        keep_kernel, [VMEM] * 3, [part, ((4, 64, 256), BF16)], [], "top_keep", 1 << 23
    )(picks, mine, keep)
    (out,) = call(
        functools.partial(top_kernel, core_axis="core"),
        [VMEM] * 9,
        [(fine_state.shape, BF16)],
        [pltpu.VMEM(*half_set), dma((4,))],
        "top_level",
        1 << 23,
        place=HBM,
    )(parcel, mixed, chosen, fine, turned, w_top_msg, w_top_agg, w_down, out_gain[None])
    return out


def solution(mesh):
    shape = dict(mesh.shape)
    inner = Mesh(
        mesh.devices.reshape(shape["ens"], shape["sy"], shape["sx"] // 2, 2),
        ("ens", "sy", "x", "core"),
    )
    sx = ("x", "core")
    in_specs = (
        P("ens", "sy", sx, None, None),
        P("sy", sx, None, None, None),
        P("sy", sx, None),
        P("sy", sx),
        P("sy", sx, None, None),
    ) + (P(),) * 12
    out_specs = P("ens", "sy", sx, None, None)
    return jax.shard_map(local, mesh=inner, in_specs=in_specs, out_specs=out_specs, check_vma=False)
```

```python
import functools

import jax
import jax.numpy as jnp
from jax import lax
from jax.experimental import pallas as pl
from jax.experimental.pallas import tpu as pltpu
from jax.sharding import Mesh, PartitionSpec as P

F32 = jnp.float32
BF16 = jnp.bfloat16
VMEM = pl.BlockSpec(memory_space=pltpu.VMEM)
HBM = pl.BlockSpec(memory_space=pltpu.HBM)
MIB = 1024 * 1024


def dot(a, b):
    return lax.dot_general(a, b, (((1,), (0,)), ((), ())), preferred_element_type=F32)


def dot_t(a, b):
    return lax.dot_general(a, b, (((0,), (0,)), ((), ())), preferred_element_type=F32)


def norm(values, gain):
    center = values - jnp.mean(values, -1, keepdims=True)
    spread = jnp.mean(center * center, -1, keepdims=True)
    return center * lax.rsqrt(spread + 1e-05) * gain


def far(array):
    return pltpu.with_memory_space_constraint(array, pltpu.HBM)


def start_all(pairs, sems):
    copies = [pltpu.make_async_copy(src, dst, sems.at[n]) for n, (src, dst) in enumerate(pairs)]
    for copy in copies:
        copy.start()
    return copies


def cut_kernel(state, map_in, last_row, first_row, last_col, first_col, up_map, sems):
    pairs = [(map_in, up_map), (state.at[:, 1:2], last_row), (state.at[:, 0:1], first_row)]
    for r in range(2):
        pairs.append((state.at[0, r, 1], last_col.at[pl.ds(128 * r, 128)]))
        pairs.append((state.at[0, r, 0], first_col.at[pl.ds(128 * r, 128)]))
    copies = start_all(pairs, sems)
    copies[0].wait()
    joins = up_map[...]
    line = lax.broadcasted_iota(jnp.int32, (16, 256), 0)
    value = jnp.zeros((16, 256), jnp.int32)
    for b in range(4):
        value = jnp.where(line == b, joins[b // 2, b % 2], value)
    value = value.astype(F32).astype(BF16)
    last_col[256:272, :] = value
    first_col[256:272, :] = value
    for copy in copies[1:]:
        copy.wait()


def stage_kernel(
    state_in, w_self_in, map_in, nbr_in, adj_in, tiles_in, w_msg_in, w_agg_in, w_out_in, gain_in,
    state, own_part, up_map, nbr, adj, tiles, w_msg, w_agg, w_out, gain, w_self, sems,
):
    pairs = [
        (state_in, state), (w_self_in, w_self), (map_in, up_map), (nbr_in, nbr), (adj_in, adj),
        (tiles_in, tiles), (w_msg_in, w_msg), (w_agg_in, w_agg), (w_out_in, w_out),
        (gain_in, gain),
    ]
    copies = start_all(pairs, sems)
    copies[0].wait()
    copies[1].wait()
    own = jnp.concatenate([state[0, b // 2, b % 2] for b in range(4)], axis=0)
    own_part[...] = dot(own, w_self[...])
    for copy in copies[2:]:
        copy.wait()


def near_kernel(
    up_map, nbr, up, down, right, left, state, adj, tiles, top_nbr_in, top_adj,
    mixed, corner_edges, label, sent, turned, keep, give, picks, frame, top_nbr, edges, sems,
    *, core_axis,
):
    table = pltpu.make_async_copy(top_nbr_in, top_nbr, sems.at[8])
    table.start()
    core = lax.axis_index(core_axis)
    joins = [up_map[...][b // 2, b % 2] for b in range(4)]
    twin = jnp.where(core == 0, right[256:272, :].astype(F32), left[256:272, :].astype(F32))
    twin = twin.astype(jnp.int32)
    joins += [twin[b, 0] for b in range(4)]
    copies = start_all([(top_adj.at[joins[b]], edges.at[b]) for b in range(8)], sems)
    for c in range(2):
        frame[1 + c] = up[0, 0, c]
        frame[13 + c] = down[0, 0, c]
        for r in range(2):
            frame[(1 + r) * 4 + 1 + c] = state[0, r, c]
    for r in range(2):
        frame[(1 + r) * 4] = left[128 * r : 128 * r + 128, :]
        frame[(1 + r) * 4 + 3] = right[128 * r : 128 * r + 128, :]
        frame[12 * r] = jnp.zeros((128, 256), BF16)
        frame[12 * r + 3] = jnp.zeros((128, 256), BF16)
    lane = lax.broadcasted_iota(jnp.int32, (64, 128), 1)
    for j in range(2):
        joined = jnp.where(lane < 64, joins[2 * j], joins[2 * j + 1])
        label[j] = jnp.where((lane & 63) == 2 * joined, 1.0, 0.0)
    row = lax.broadcasted_iota(jnp.int32, (128, 128), 0)
    col = lax.broadcasted_iota(jnp.int32, (128, 128), 1)
    want = (row & 1) * 64 + (row & 62) + (row >> 6)
    order = jnp.where(col == want, 1.0, 0.0).astype(BF16)
    for y in range(2):
        for x in range(2):
            b = 2 * y + x
            picked = []
            for k in range(4):
                code = nbr[y][x, k]
                spot = (y + lax.div(code, 3)) * 4 + x + lax.rem(code, 3)
                picked.append(frame[spot])
                tile = adj[y, x, k]
                corner = jnp.where(code == 6 * y + 2 * x, tile, jnp.zeros_like(tile))
                joint = corner.astype(F32) if k == 0 else joint + corner.astype(F32)
            corner_edges[b] = joint.astype(BF16)
            tile_row = jnp.concatenate([adj[y, x, k] for k in range(4)], axis=1)
            mixed[128 * b : 128 * b + 128] = dot(tile_row, jnp.concatenate(picked, axis=0))
    for b in range(4):
        turned[b // 2, b % 2] = tiles[b // 2, b % 2].T
        sent[b] = dot(order, tiles[b // 2, b % 2]).astype(BF16)
    for b in range(8):
        copies[b].wait()
        low = jnp.concatenate([edges[b, k][:, :64] for k in range(4)], axis=1)
        high = jnp.concatenate([edges[b, k][:, 64:] for k in range(4)], axis=1)
        (keep if b < 4 else give)[b % 4] = jnp.where(core == 1, low, high)
    table.wait()
    for b in range(8):
        picks[pl.ds(b, 1), :] = jnp.full((1, 128), joins[b], jnp.int32)
        for k in range(4):
            source = jnp.full((1, 128), top_nbr[k, joins[b]], jnp.int32)
            picks[pl.ds(8 + 4 * b + k, 1), :] = source


def fine_kernel(
    corner_l, corner_r, mixed_in, corner_edges, label, sent, state, own_part,
    w_msg, w_agg, w_out, gain, fine_out, piece_out, lines,
):
    own, mixed = [], []
    for y in range(2):
        for x in range(2):
            b = 2 * y + x
            corner = (corner_r if x else corner_l)[1 - y]
            total = mixed_in[128 * b : 128 * b + 128] + dot(corner_edges[b], corner)
            mixed.append(total.astype(BF16))
            own.append(state[0, y, x])
    own = jnp.concatenate(own, axis=0)
    mixed = jnp.concatenate(mixed, axis=0)
    agg = dot(mixed, w_msg[...]).astype(BF16)
    hidden = jax.nn.silu(own_part[...] + dot(agg, w_agg[...])).astype(BF16)
    fine = norm(own.astype(F32) + dot(hidden, w_out[...]), gain[...]).astype(BF16)
    fine_out[...] = fine
    for b in range(4):
        contrib = dot(sent[b], fine[b * 128 : (b + 1) * 128])
        for h in range(2):
            for i in range(2):
                part = contrib[64 * i : 64 * i + 64, 128 * h : 128 * h + 128]
                lines[pl.ds(8 * h + 2 * b + i, 64, stride=18), :] = part
    for j in range(2):
        lines[pl.ds(16 + j, 64, stride=18), :] = label[j]
    piece_out[...] = lines[0:1152, :].astype(BF16)


def sum_kernel(got, gain, share_out, lines):
    lines[0:1152, :] = got[...].astype(F32)
    take = lambda n: lines[pl.ds(n, 64, stride=18), :]
    labels = [take(16), take(17)]
    member, values = [], []
    for b in range(4):
        for i in range(2):
            turn = 64 * (b % 2) + i
            member.append(pltpu.roll(labels[b // 2], turn, 1) if turn else labels[b // 2])
            wide = [take(8 * h + 2 * b + i) for h in range(2)]
            values.append(jnp.concatenate(wide, axis=1))
    member = jnp.concatenate(member, axis=0).astype(BF16)
    values = jnp.concatenate(values, axis=0).astype(BF16)
    total = dot_t(member, values)[:40]
    share = norm(total, gain[...]).astype(BF16)
    share_out[...] = jnp.broadcast_to(share[None], share_out.shape)


def order_kernel(got, out):
    row = lax.broadcasted_iota(jnp.int32, (160, 160), 0)
    col = lax.broadcasted_iota(jnp.int32, (160, 160), 1)
    want = ((row & 7) >> 1) * 40 + (row >> 3) * 2 + (row & 1)
    order = jnp.where(col == want, 1.0, 0.0).astype(BF16)
    moved = [dot(order, got[4 * h : 4 * h + 4].reshape(160, 256)) for h in range(2)]
    moved = jnp.concatenate([part.reshape(20, 8, 256) for part in moved], axis=1)
    out[...] = jnp.broadcast_to(moved.astype(BF16)[None], out.shape)


def half_block(source, at):
    return jnp.concatenate([source[x, at] for x in range(4)], axis=0)


def pick(picks, line):
    return picks[pl.ds(line, 1), pl.ds(0, 1)][0, 0]


def gather_parts(picks, first, edges, source):
    mixed = []
    for b in range(4):
        lines = [8 + 4 * (first + b) + k for k in range(4)]
        picked = [half_block(source, pick(picks, line)) for line in lines]
        mixed.append(dot(edges[b], jnp.concatenate(picked, axis=0)))
    return jnp.concatenate(mixed, axis=0)


def give_kernel(picks, mine, give, parcel):
    for b in range(4):
        parcel[512 + 64 * b : 576 + 64 * b, :] = half_block(mine, pick(picks, 4 + b))
    parcel[0:512, :] = gather_parts(picks, 4, give, mine).astype(BF16)


def keep_kernel(picks, mine, keep, mixed, chosen):
    for b in range(4):
        chosen[b] = half_block(mine, pick(picks, b))
    mixed[...] = gather_parts(picks, 0, keep, mine)


def top_kernel(
    parcel, mixed, chosen, fine, turned, w_msg, w_agg, w_down, gain, out, whole, sems, *, core_axis
):
    core = lax.axis_index(core_axis)
    here = pl.ds(pl.multiple_of((1 - core) * 64, 64), 64)
    there = pl.ds(pl.multiple_of(core * 64, 64), 64)
    for b in range(4):
        whole[b, here, :] = chosen[b]
        whole[b, there, :] = parcel[512 + 64 * b : 576 + 64 * b, :]
    both = mixed[...] + parcel[0:512, :].astype(F32)
    tagg = dot(both.astype(BF16), w_msg[...]).astype(BF16)
    zero = jnp.concatenate([whole[b] for b in range(4)], axis=0).astype(F32)
    one = (zero + jax.nn.silu(dot(tagg, w_agg[...]))).astype(BF16)
    copies = []
    for b in range(4):
        rows = slice(b * 128, (b + 1) * 128)
        lower = dot(turned[b // 2, b % 2], one[rows]).astype(BF16)
        final = norm(fine[rows].astype(F32) + dot(lower, w_down[...]), gain[...])
        whole[b] = final.astype(BF16)
        copy = pltpu.make_async_copy(whole.at[b], out.at[0, b // 2, b % 2], sems.at[b])
        copy.start()
        copies.append(copy)
    for copy in copies:
        copy.wait()


def call(body, ins, outs, scratch, name, busy=0, limit=24, place=VMEM):
    return pl.pallas_call(
        body,
        out_shape=tuple(jax.ShapeDtypeStruct(shape, kind) for shape, kind in outs),
        in_specs=ins,
        out_specs=(place,) * len(outs),
        scratch_shapes=scratch,
        compiler_params=pltpu.CompilerParams(vmem_limit_bytes=limit * MIB),
        cost_estimate=pl.CostEstimate(flops=0, bytes_accessed=busy, transcendentals=0),
        name=name,
    )


def local(
    fine_state, fine_adj, fine_nbr, up_map, up_tiles, top_adj, top_nbr, w_fine_msg, w_fine_self,
    w_fine_agg, w_fine_out, w_top_msg, w_top_agg, w_down, fine_gain, top_gain, out_gain,
):
    sx = ("x", "core")
    rows, cols = lax.axis_size("sy"), lax.axis_size("x") * lax.axis_size("core")
    east = [(i, (i + 1) % cols) for i in range(cols)]
    west = [(j, i) for i, j in east]
    twin = [(0, 1), (1, 0)]
    south = [(i, i + 1) for i in range(rows - 1)]
    north = [(j, i) for i, j in south]
    weight = ((256, 256), BF16)
    tile_set = ((2, 2, 128, 128), BF16)
    part = ((512, 256), F32)
    gain = ((1, 256), F32)
    row_cut, col_cut = ((1, 1, 2, 128, 256), BF16), ((272, 256), BF16)
    dma = pltpu.SemaphoreType.DMA
    last_row, first_row, last_col, first_col = call(
        cut_kernel,
        [HBM] * 2,
        [row_cut, row_cut, col_cut, col_cut],
        [pltpu.VMEM((2, 2), jnp.int32), dma((7,))],
        "cut",
        1 << 20,
    )(far(fine_state), far(up_map))
    down = lax.ppermute(first_row, "sy", north)
    up = lax.ppermute(last_row, "sy", south)
    left = lax.ppermute(last_col, sx, east)
    right = lax.ppermute(first_col, sx, west)
    half_set = ((4, 128, 256), BF16)
    staged = [
        up_map, fine_nbr, fine_adj, up_tiles, w_fine_msg, w_fine_agg, w_fine_out, fine_gain[None],
    ]
    held = call(
        stage_kernel,
        [HBM] * 10,
        [(fine_state.shape, BF16), part] + [(array.shape, array.dtype) for array in staged],
        [pltpu.VMEM(*weight), dma((10,))],
        "stage",
        1 << 23,
    )(*[far(array) for array in [fine_state, w_fine_self] + staged])
    down, up, held = lax.optimization_barrier((down, up, held))
    corner_l = lax.ppermute(jnp.concatenate([down[0, :, 1], up[0, :, 1]]), sx, east)
    corner_r = lax.ppermute(jnp.concatenate([down[0, :, 0], up[0, :, 0]]), sx, west)
    state, own_part, map_here, nbr_here, adj, tiles, *weights = held
    mixed, corner_edges, label, sent, turned, keep, give, picks = call(
        functools.partial(near_kernel, core_axis="core"),
        [VMEM] * 9 + [HBM] * 2,
        [
            part, ((4, 128, 128), BF16), ((2, 64, 128), F32), ((4, 128, 128), BF16), tile_set,
            half_set, half_set, ((40, 128), jnp.int32),
        ],
        [
            pltpu.VMEM((16, 128, 256), BF16), pltpu.SMEM((4, 20), jnp.int32),
            pltpu.VMEM((8, 4, 128, 128), BF16), dma((9,)),
        ],
        "near",
        1 << 23,
    )(map_here, nbr_here, up, down, right, left, state, adj, tiles, far(top_nbr.T), far(top_adj))
    fine, piece = call(
        fine_kernel,
        [VMEM] * 12,
        [((512, 256), BF16), ((64 * 18, 128), BF16)],
        [pltpu.VMEM((64 * 18 + 24, 128), F32)],
        "fine_level",
        1 << 23,
    )(corner_l, corner_r, mixed, corner_edges, label, sent, state, own_part, *weights)
    piece = piece.reshape(64, 9, 2, 128)
    chips = lax.axis_size("x") * rows
    back = [2 * chip + core for chip in range(chips - 1, -1, -1) for core in (1, 0)]
    got = lax.all_to_all(piece, ("x", "sy", "core"), 0, 0, axis_index_groups=[back])
    (share,) = call(
        sum_kernel,
        [VMEM] * 2,
        [((8, 40, 256), BF16)],
        [pltpu.VMEM((64 * 18 + 24, 128), F32)],
        "top_sum",
        1 << 20,
    )(got.reshape(64 * 18, 128), top_gain[None])
    column = lax.all_to_all(share, "sy", 0, 0, axis_index_groups=[list(range(rows - 1, -1, -1))])
    (column,) = call(
        order_kernel, [VMEM], [((4, 20, 16, 256), BF16)], [], "top_order", 1 << 20
    )(column)
    mine = lax.all_to_all(column, "x", 0, 0, axis_index_groups=[list(range(cols // 2 - 1, -1, -1))])
    (parcel,) = call(
        give_kernel, [VMEM] * 3, [((768, 256), BF16)], [], "top_give", 1 << 20
    )(picks, mine, give)
    parcel = lax.ppermute(parcel, "core", twin)
    mixed, chosen = call(
        keep_kernel, [VMEM] * 3, [part, ((4, 64, 256), BF16)], [], "top_keep", 1 << 23
    )(picks, mine, keep)
    (out,) = call(
        functools.partial(top_kernel, core_axis="core"),
        [VMEM] * 9,
        [(fine_state.shape, BF16)],
        [pltpu.VMEM(*half_set), dma((4,))],
        "top_level",
        1 << 23,
        place=HBM,
    )(parcel, mixed, chosen, fine, turned, w_top_msg, w_top_agg, w_down, out_gain[None])
    return out


def solution(mesh):
    shape = dict(mesh.shape)
    inner = Mesh(
        mesh.devices.reshape(shape["ens"], shape["sy"], shape["sx"] // 2, 2),
        ("ens", "sy", "x", "core"),
    )
    sx = ("x", "core")
    in_specs = (
        P("ens", "sy", sx, None, None),
        P("sy", sx, None, None, None),
        P("sy", sx, None),
        P("sy", sx),
        P("sy", sx, None, None),
    ) + (P(),) * 12
    out_specs = P("ens", "sy", sx, None, None)
    return jax.shard_map(local, mesh=inner, in_specs=in_specs, out_specs=out_specs, check_vma=False)
```
